32 devices in a mesh: dp: 8 (over z, y), vocab: 4 (over x, core).
Axes of the slice: x: 2, y: 2, z: 4, core: 2. Of those that a mesh axis runs over, the one named last changes fastest.
Arguments:
- hidden_rows: bfloat16 [2048, 5120], P('dp'), may hold values from -300 to 300, as said below
- plan_lengths: int32 [8], replicated, may hold values from 1 to 256, 1024 in all
- shard_of_class: int32 [8], replicated, may hold values from 0 to 7, each once
- head_weight: bfloat16 [5120, 3072], P(None, 'vocab'), may hold values from -0.078125 to 0.078125
- teacher_logprobs: bfloat16 [1024, 3072], P('dp', 'vocab'), as said below
Outputs:
- row_grad: bfloat16 [2048, 5120], P('dp')
- row_kl: float32 [1024], P('dp')
The draws below stay inside these ranges and needn't reach their ends.
Inputs may be any that keep to these rules, and one draw needn't show every extreme that they name: `plan_lengths`: the plan lengths sum to 1024 and the longest is exactly 256. `shard_of_class`: each shard is named once. `hidden_rows`: unused slots hold finite values. `teacher_logprobs`: each row is a log-softmax over the 3072 entries, rounded to bfloat16.
All inputs are finite; a program needn't handle non-finite values.
Results may differ from the reference program's by a relative error of at most 0.0046.
Values may be sent and summed in bfloat16 or wider, within the bound.
A program may use at most 64 MiB of HBM per device.

```python
import math
import jax
import jax.numpy as jnp
import numpy as np
from jax import lax

D = 5120
ROW_BAL = 128
SRC_CAP = 256
TOKENS = 1024
TOKENS_CAP = 2048
VOCAB = 3072
N_DP = 8


def draw_hidden_rows(key, part):
    first, second = jax.random.split(jax.random.fold_in(key, 11), 2)
    base = jnp.clip(jax.random.normal(first, (TOKENS_CAP, D), jnp.float32), -5.0, 5.0)
    scales = jnp.exp(jax.random.uniform(second, (TOKENS_CAP, 1), jnp.float32, 0.0, math.log(10.0)))
    values = base * scales
    return jnp.clip(values, -300.0, 300.0).astype(jnp.bfloat16)


def draw_teacher_logprobs(key, part):
    first = jax.random.fold_in(jax.random.fold_in(key, 23), 0)
    logits = 3.0 * jnp.clip(jax.random.normal(first, (TOKENS, VOCAB), jnp.float32), -6.0, 6.0)
    logprobs = logits - jax.scipy.special.logsumexp(logits, axis=1, keepdims=True)
    return logprobs.astype(jnp.bfloat16)


def block_scale(rng, shape, pieces, low, largest):
    def one(dim, shards_of):
        heights = jax.random.uniform(jax.random.fold_in(jax.random.fold_in(rng, 6), dim), (shards_of,), jnp.float32, low / len(pieces), largest / len(pieces))
        return jnp.repeat(jnp.exp(heights), shape[dim] // shards_of).reshape((-1,) + (1,) * (len(shape) - dim - 1))

    gain = one(*pieces[0])
    for cut in pieces[1:]:
        gain = gain * one(*cut)
    return gain


def length_profile(number_of, total, bound, slope):
    loads = [(1 << 20) // math.isqrt(standing ** slope) + 1 for standing in range(2, number_of + 1)]
    surplus, counts = total - bound - (number_of - 1), [1] * (number_of - 1)
    while surplus > 0:
        candidates = [i for i in range(number_of - 1) if counts[i] < bound]
        mass, budget = sum([loads[i] for i in candidates]), surplus
        for i in candidates:
            extra = min(bound - counts[i], max(1, budget * loads[i] // mass), surplus)
            counts[i] = counts[i] + extra
            surplus = surplus - extra
    return np.array([bound] + counts)


def ragged_sizes(key, number_of, total, bound, skew):
    if number_of == 2:
        one = jax.random.randint(key, (), max(1, total - bound), min(bound, total - 1) + 1)
        return jnp.stack([one, total - one])
    sizes = jnp.asarray(length_profile(number_of, total, bound, skew), jnp.int32)
    couples = (number_of - 1) // 2
    source_of, taker = sizes[1:1 + 2 * couples:2], sizes[2:2 + 2 * couples:2]
    margin = jnp.minimum(source_of - 1, bound - taker)
    passed = jax.random.randint(jax.random.fold_in(key, 1), (couples,), 0, 1 << 20) % (margin + 1)
    sizes = sizes.at[1:1 + 2 * couples:2].set(source_of - passed).at[2:2 + 2 * couples:2].set(taker + passed)
    return sizes[jax.random.permutation(jax.random.fold_in(key, 2), number_of)]


def gaussian(stream_key, dims, deviation, bound, cuts=(), kind=jnp.bfloat16):
    drawn = deviation * jax.random.normal(stream_key, dims, jnp.float32)
    if cuts:
        drawn = drawn * block_scale(stream_key, dims, cuts, -0.22, 0.18)
    return jnp.clip(drawn, -bound, bound).astype(kind)


def setup_inputs(seed: int = 0) -> dict:
    seeds = jax.random.split(jax.random.key(seed), 6)
    return {
        "hidden_rows": draw_hidden_rows(jax.random.fold_in(seeds[5], 71), 0),
        "plan_lengths": ragged_sizes(seeds[1], N_DP, TOKENS, SRC_CAP, 2).astype(jnp.int32),
        "shard_of_class": jax.random.permutation(seeds[2], N_DP).astype(jnp.int32),
        "head_weight": gaussian(seeds[3], (D, VOCAB), D ** -0.5, 0.078125, ((1, 4),)),
        "teacher_logprobs": draw_teacher_logprobs(jax.random.fold_in(seeds[5], 71), 0),
    }


loss_scale = 64.0


def divergence(row_block, teacher_block, weight):
    logits = jnp.dot(row_block, weight, preferred_element_type=jnp.float32)
    row_top = jnp.max(logits, axis=1, keepdims=True)
    log_total = row_top + jnp.log(jnp.sum(jnp.exp(logits - row_top), axis=1, keepdims=True))
    log_teacher = teacher_block.astype(jnp.float32)
    teacher_prob = jnp.exp(log_teacher)
    prob_total = jnp.sum(teacher_prob, axis=1, keepdims=True)
    row_div = jnp.sum(teacher_prob * (log_teacher - logits), axis=1) + prob_total[:, 0] * log_total[:, 0]
    grad_logits = (loss_scale * (prob_total * jnp.exp(logits - log_total) - teacher_prob)).astype(jnp.bfloat16)
    hidden_grad = jnp.dot(grad_logits, weight.T, preferred_element_type=jnp.float32).astype(jnp.bfloat16)
    return row_div, hidden_grad


def reference(hidden_rows, plan_lengths, shard_of_class, head_weight, teacher_logprobs):
    shards = N_DP
    lengths = plan_lengths.astype(jnp.int32)
    offsets = (jnp.cumsum(lengths) - lengths).astype(jnp.int32)
    classes = jnp.arange(shards, dtype=jnp.int32)
    inverse = jnp.sum(jnp.where(shard_of_class[None, :] == classes[:, None], classes[None, :], 0), axis=1).astype(jnp.int32)
    slot_index = jnp.arange(ROW_BAL, dtype=jnp.int32)

    def one_shard(shard_index):
        packed_index = (slot_index * shards + inverse[shard_index]).astype(jnp.int32)
        owner = (jnp.sum((offsets[None, :] <= packed_index[:, None]).astype(jnp.int32), axis=1) - 1).astype(jnp.int32)
        source_row = (owner * SRC_CAP + packed_index - offsets[owner]).astype(jnp.int32)
        row_block = hidden_rows[source_row]
        teacher_block = lax.dynamic_slice_in_dim(teacher_logprobs, (shard_index * ROW_BAL).astype(jnp.int32), ROW_BAL, 0)
        row_div, hidden_grad = divergence(row_block, teacher_block, head_weight)
        return row_div, hidden_grad, source_row

    row_divs, grads, source_rows = lax.map(one_shard, classes)
    row_kl = row_divs.reshape(-1)
    row_grad = jnp.zeros((TOKENS_CAP, D), jnp.bfloat16).at[source_rows.reshape(-1)].set(grads.reshape(-1, D))
    return row_grad, row_kl
```

```python
import functools

import jax
import jax.numpy as jnp
from jax import lax
from jax.experimental import pallas as pl
from jax.experimental.pallas import tpu as pltpu
from jax.sharding import PartitionSpec as P

loss_scale = 64.0
MESH = pl.DeviceIdType.MESH
GROUPS = 2
KBLK = 512
CBLK = 512


def kernel(
    n,
    nv,
    len_ref,
    soc_ref,
    teach_ref,
    hid_hbm,
    w_hbm,
    out_hbm,
    kl_ref,
    w_v,
    h_v,
    z_v,
    q_v,
    g_v,
    tout,
    tin,
    st,
    klb,
    sib_out,
    sib_in,
    xs,
    xr,
    fin,
    w_sem,
    h_sem,
    ts_sem,
    tr_sem,
    tl_sem,
    ss_sem,
    sr_sem,
    ks_sem,
    kr_sem,
    bs_sem,
    br_sem,
    xs_sem,
    xr_sem,
    fs_sem,
    fr_sem,
    fl_sem,
):
    me = lax.axis_index("dp")
    v = lax.axis_index("vocab")
    core = lax.rem(v, 2)
    sib = v + 1 - 2 * core
    across = lax.rem(v + 2, 4)
    slots, feat = hid_hbm.shape
    bal, vloc = teach_ref.shape
    steps = feat // KBLK
    rows = slots // GROUPS
    half = feat // 2
    chunks = half // CBLK
    per = rows // n
    dep = tin.shape[2]
    shift = n.bit_length() - 1

    barrier = pltpu.get_barrier_semaphore()
    for k in range(1, n):
        pl.semaphore_signal(barrier, 1, device_id=(lax.rem(me + k, n), v), device_id_type=MESH)
    for k in range(1, nv):
        pl.semaphore_signal(barrier, 1, device_id=(me, lax.rem(v + k, nv)), device_id_type=MESH)

    def w_load(k):
        return pltpu.make_async_copy(
            w_hbm.at[pl.ds(pl.multiple_of(k * KBLK, KBLK), KBLK), :],
            w_v.at[pl.ds(pl.multiple_of(k * KBLK, KBLK), KBLK), :],
            w_sem.at[k],
        )

    def h_load(k):
        return pltpu.make_async_copy(
            hid_hbm.at[:, pl.ds(pl.multiple_of(k * KBLK, KBLK), KBLK)], h_v.at[k], h_sem.at[k]
        )

    @pl.loop(0, steps)
    def _(k):
        w_load(k).start()
        h_load(k).start()

    lens, offs, run = [], [], jnp.int32(0)
    for s in range(n):
        ln = len_ref[s]
        lens.append(ln)
        offs.append(run)
        run = run + ln
    zero = jnp.int32(0)
    inv_me, off_me, len_me = zero, zero, zero
    for s in range(n):
        inv_me = inv_me + jnp.where(soc_ref[s] == me, jnp.int32(s), zero)
        off_me = off_me + jnp.where(me == s, offs[s], zero)
        len_me = len_me + jnp.where(me == s, lens[s], zero)

    for g in range(GROUPS):
        for s in range(n):
            b0 = lax.shift_right_logical(offs[s] + ((inv_me - offs[s]) & (n - 1)), shift)
            first = b0 + g * per
            r = lax.broadcasted_iota(jnp.int32, (dep, bal), 0)
            b = lax.broadcasted_iota(jnp.int32, (dep, bal), 1)
            hot = jnp.where(b == r + first, 1.0, 0.0).astype(jnp.bfloat16)
            tout[g, s] = jnp.dot(
                hot, teach_ref[...], preferred_element_type=jnp.float32
            ).astype(jnp.bfloat16)

    def t_send(g, to):
        return pltpu.make_async_remote_copy(
            src_ref=tout.at[g, to],
            dst_ref=tin.at[g, me],
            send_sem=ts_sem.at[g, to],
            recv_sem=tr_sem.at[g, me],
            device_id=(to, v),
            device_id_type=MESH,
        )

    def t_recv(g, frm):
        return pltpu.make_async_remote_copy(
            src_ref=tout.at[g, frm],
            dst_ref=tin.at[g, frm],
            send_sem=ts_sem.at[g, frm],
            recv_sem=tr_sem.at[g, frm],
            device_id=(frm, v),
            device_id_type=MESH,
        )

    def t_own(g):
        return pltpu.make_async_copy(tout.at[g, me], tin.at[g, me], tl_sem.at[g])

    pl.semaphore_wait(barrier, n - 1 + nv - 1)
    for g in range(GROUPS):
        t_own(g).start()

        @pl.loop(1, n)
        def _(k):
            t_send(g, lax.rem(me + k, n)).start()

    z_v[...] = jnp.zeros_like(z_v)

    @pl.loop(0, steps)
    def _(k):
        w_load(k).wait()
        h_load(k).wait()
        z_v[...] += jnp.dot(
            h_v[k],
            w_v[pl.ds(pl.multiple_of(k * KBLK, KBLK), KBLK), :],
            preferred_element_type=jnp.float32,
        )

    def s_copy(g, frm, to):
        return pltpu.make_async_remote_copy(
            src_ref=st.at[g, frm],
            dst_ref=st.at[g, frm],
            send_sem=ss_sem.at[g, to],
            recv_sem=sr_sem.at[g, frm],
            device_id=(me, to),
            device_id_type=MESH,
        )

    def b_copy(g, j):
        return pltpu.make_async_remote_copy(
            src_ref=sib_out.at[g, j],
            dst_ref=sib_in.at[g, j],
            send_sem=bs_sem.at[g, j],
            recv_sem=br_sem.at[g, j],
            device_id=(me, sib),
            device_id_type=MESH,
        )

    def x_copy(g, j):
        return pltpu.make_async_remote_copy(
            src_ref=xs.at[g, j],
            dst_ref=xr.at[g, j],
            send_sem=xs_sem.at[g, j],
            recv_sem=xr_sem.at[g, j],
            device_id=(me, across),
            device_id_type=MESH,
        )

    def place(g, owner, j):
        col = pl.multiple_of(owner * half + j * CBLK, 128)
        return out_hbm.at[pl.ds(g * rows, rows), pl.ds(col, CBLK)]

    def f_send(g, j):
        return pltpu.make_async_remote_copy(
            src_ref=fin.at[g, j],
            dst_ref=place(g, core, j),
            send_sem=fs_sem.at[g, j],
            recv_sem=fr_sem.at[g, j],
            device_id=(me, sib),
            device_id_type=MESH,
        )

    def f_recv(g, j):
        return pltpu.make_async_remote_copy(
            src_ref=fin.at[g, j],
            dst_ref=place(g, 1 - core, j),
            send_sem=fs_sem.at[g, j],
            recv_sem=fr_sem.at[g, j],
            device_id=(me, sib),
            device_id_type=MESH,
        )

    def f_own(g, j):
        return pltpu.make_async_copy(fin.at[g, j], place(g, core, j), fl_sem.at[g, j])

    def w_rows(owner, j):
        return w_v[pl.ds(pl.multiple_of(owner * half + j * CBLK, CBLK), CBLK), :]

    def back(g, owner, j):
        return lax.dot_general(
            g_v[pl.ds(g * rows, rows), :],
            w_rows(owner, j),
            (((1,), (1,)), ((), ())),
            preferred_element_type=jnp.float32,
        )

    for g in range(GROUPS):
        span = pl.ds(g * rows, rows)
        slot = lax.broadcasted_iota(jnp.int32, (rows, 1), 0) + g * rows
        live = slot < len_me
        cls = (off_me + slot) & (n - 1)
        owner = jnp.zeros((rows, 1), jnp.int32)
        for c in range(n):
            owner = owner + jnp.where(cls == c, soc_ref[c], zero)
        rank = lax.shift_right_logical(slot, shift) - g * per
        pick = owner * dep + rank
        lane = lax.broadcasted_iota(jnp.int32, (rows, n * dep), 1)
        hot = jnp.where(lane == pick, 1.0, 0.0).astype(jnp.bfloat16)

        t_own(g).wait()

        @pl.loop(1, n)
        def _(k):
            t_recv(g, lax.rem(me + k, n)).wait_recv()

        t = jnp.dot(
            hot, tin[g].reshape(n * dep, vloc), preferred_element_type=jnp.float32
        )
        z = jnp.where(live, z_v[span, :], 0.0)
        q = jnp.exp(t)
        q_v[span, :] = q
        top = jnp.max(z, axis=1, keepdims=True)
        total = jnp.sum(jnp.exp(z - top), axis=1, keepdims=True)
        mass = jnp.sum(q, axis=1, keepdims=True)
        cross = jnp.sum(q * (t - z), axis=1, keepdims=True)
        col = lax.broadcasted_iota(jnp.int32, (rows, 128), 1)
        packed = jnp.where(
            col == 0, top, jnp.where(col == 1, total, jnp.where(col == 2, mass, cross))
        )
        st[g, v] = packed.T[:8, :]

        @pl.loop(1, nv)
        def _(k):
            s_copy(g, v, lax.rem(v + k, nv)).start()

        @pl.loop(1, nv)
        def _(k):
            frm = lax.rem(v + k, nv)
            s_copy(g, frm, frm).wait_recv()

        peak = st[g, 0, 0:1, :]
        for u in range(1, nv):
            peak = jnp.maximum(peak, st[g, u, 0:1, :])
        sums = jnp.zeros_like(peak)
        masses = jnp.zeros_like(peak)
        crosses = jnp.zeros_like(peak)
        for u in range(nv):
            sums = sums + st[g, u, 1:2, :] * jnp.exp(st[g, u, 0:1, :] - peak)
            masses = masses + st[g, u, 2:3, :]
            crosses = crosses + st[g, u, 3:4, :]
        lse = peak + jnp.log(sums)
        klb[me, :, pl.ds(g * rows, rows)] = jnp.broadcast_to(crosses + masses * lse, (8, rows))
        sub = lax.broadcasted_iota(jnp.int32, (128, rows), 0)
        back_cols = jnp.where(sub == 0, lse, masses).T
        lse_c = back_cols[:, 0:1]
        mass_c = back_cols[:, 1:2]
        z = jnp.where(live, z_v[span, :], 0.0)
        grad = loss_scale * (mass_c * jnp.exp(z - lse_c) - q_v[span, :])
        g_v[span, :] = jnp.where(live, grad, 0.0).astype(jnp.bfloat16)

        @pl.loop(0, chunks)
        def _(j):
            sib_out[g, j] = back(g, 1 - core, j)
            b_copy(g, j).start()

        @pl.loop(0, chunks)
        def _(j):
            mine = back(g, core, j)
            b_copy(g, j).wait_recv()
            xs[g, j] = (mine + sib_in[g, j]).astype(jnp.bfloat16)
            x_copy(g, j).start()

    def k_copy(frm, to):
        return pltpu.make_async_remote_copy(
            src_ref=klb.at[frm],
            dst_ref=klb.at[frm],
            send_sem=ks_sem.at[to],
            recv_sem=kr_sem.at[frm],
            device_id=(to, v),
            device_id_type=MESH,
        )

    @pl.loop(1, n)
    def _(k):
        k_copy(me, lax.rem(me + k, n)).start()

    @pl.loop(1, n)
    def _(k):
        frm = lax.rem(me + k, n)
        k_copy(frm, frm).wait_recv()

    want = lax.broadcasted_iota(jnp.int32, (bal, slots), 0) * n + inv_me
    inner = lax.broadcasted_iota(jnp.int32, (bal, slots), 1)
    acc = jnp.zeros((bal, slots), jnp.float32)
    for s in range(n):
        hit = (want - offs[s] == inner) & (inner < lens[s])
        acc = jnp.where(hit, klb[s, 0:1, :], acc)
    kl_col = jnp.sum(acc, axis=1, keepdims=True)
    diag = lax.broadcasted_iota(jnp.int32, (bal, bal), 0) == lax.broadcasted_iota(
        jnp.int32, (bal, bal), 1
    )
    kl_ref[...] = jnp.sum(jnp.where(diag, kl_col, 0.0), axis=0, keepdims=True)

    for g in range(GROUPS):

        @pl.loop(0, chunks)
        def _(j):
            x_copy(g, j).wait_recv()
            fin[g, j] = (xs[g, j].astype(jnp.float32) + xr[g, j].astype(jnp.float32)).astype(
                jnp.bfloat16
            )
            f_send(g, j).start()
            f_own(g, j).start()

    for g in range(GROUPS):

        @pl.loop(1, n)
        def _(k):
            t_send(g, lax.rem(me + k, n)).wait_send()

        @pl.loop(1, nv)
        def _(k):
            s_copy(g, v, lax.rem(v + k, nv)).wait_send()

        @pl.loop(0, chunks)
        def _(j):
            b_copy(g, j).wait_send()
            x_copy(g, j).wait_send()
            f_send(g, j).wait_send()
            f_own(g, j).wait()
            f_recv(g, j).wait_recv()

    @pl.loop(1, n)
    def _(k):
        k_copy(me, lax.rem(me + k, n)).wait_send()


def body(hidden_rows, plan_lengths, shard_of_class, head_weight, teacher_logprobs):
    n = lax.axis_size("dp")
    nv = lax.axis_size("vocab")
    slots, feat = hidden_rows.shape
    bal, vloc = teacher_logprobs.shape
    steps = feat // KBLK
    rows = slots // GROUPS
    chunks = feat // 2 // CBLK
    dep = max(16, rows // n)
    dma = pltpu.SemaphoreType.DMA
    bf, f32 = jnp.bfloat16, jnp.float32
    flops = 4 * slots * feat * vloc
    row_grad, row_kl = pl.pallas_call(
        functools.partial(kernel, n, nv),
        out_shape=(
            jax.ShapeDtypeStruct((slots, feat), bf),
            jax.ShapeDtypeStruct((1, bal), f32),
        ),
        in_specs=[
            pl.BlockSpec(memory_space=pltpu.SMEM),
            pl.BlockSpec(memory_space=pltpu.SMEM),
            pl.BlockSpec(memory_space=pltpu.VMEM),
            pl.BlockSpec(memory_space=pl.ANY),
            pl.BlockSpec(memory_space=pl.ANY),
        ],
        out_specs=(
            pl.BlockSpec(memory_space=pl.ANY),
            pl.BlockSpec(memory_space=pltpu.VMEM),
        ),
        scratch_shapes=[
            pltpu.VMEM((feat, vloc), bf),
            pltpu.VMEM((steps, slots, KBLK), bf),
            pltpu.VMEM((slots, vloc), f32),
            pltpu.VMEM((slots, vloc), f32),
            pltpu.VMEM((slots, vloc), bf),
            pltpu.VMEM((GROUPS, n, dep, vloc), bf),
            pltpu.VMEM((GROUPS, n, dep, vloc), bf),
            pltpu.VMEM((GROUPS, nv, 8, rows), f32),
            pltpu.VMEM((n, 8, slots), f32),
            pltpu.VMEM((GROUPS, chunks, rows, CBLK), f32),
            pltpu.VMEM((GROUPS, chunks, rows, CBLK), f32),
            pltpu.VMEM((GROUPS, chunks, rows, CBLK), bf),
            pltpu.VMEM((GROUPS, chunks, rows, CBLK), bf),
            pltpu.VMEM((GROUPS, chunks, rows, CBLK), bf),
            dma((steps,)),
            dma((steps,)),
            dma((GROUPS, n)),
            dma((GROUPS, n)),
            dma((GROUPS,)),
            dma((GROUPS, nv)),
            dma((GROUPS, nv)),
            dma((n,)),
            dma((n,)),
            dma((GROUPS, chunks)),
            dma((GROUPS, chunks)),
            dma((GROUPS, chunks)),
            dma((GROUPS, chunks)),
            dma((GROUPS, chunks)),
            dma((GROUPS, chunks)),
            dma((GROUPS, chunks)),
        ],
        compiler_params=pltpu.CompilerParams(
            collective_id=0, has_side_effects=True, vmem_limit_bytes=50 * 1024 * 1024
        ),
        cost_estimate=pl.CostEstimate(
            flops=flops, bytes_accessed=2 * feat * (vloc + 2 * slots), transcendentals=3 * slots * vloc
        ),
        name="plan_loss",
    )(plan_lengths, shard_of_class, teacher_logprobs, hidden_rows, head_weight)
    return row_grad, row_kl.reshape(bal)


def solution(mesh):
    return jax.shard_map(
        body,
        mesh=mesh,
        in_specs=(P("dp", None), P(), P(), P(None, "vocab"), P("dp", "vocab")),
        out_specs=(P("dp", None), P("dp")),
        check_vma=False,
    )
```

```python
import functools

import jax
import jax.numpy as jnp
from jax import lax
from jax.experimental import pallas as pl
from jax.experimental.pallas import tpu as pltpu
from jax.sharding import PartitionSpec as P

loss_scale = 64.0
MESH = pl.DeviceIdType.MESH
GROUPS = 2
KBLK = 512
CBLK = 512


def kernel(
    n,
    nv,
    len_hbm,
    soc_hbm,
    teach_hbm,
    hid_hbm,
    w_hbm,
    out_hbm,
    kl_ref,
    len_ref,
    soc_ref,
    teach_ref,
    w_v,
    w_sib,
    h_v,
    z_v,
    q_v,
    g_v,
    tout,
    tin,
    st,
    klb,
    g_sib,
    xs,
    xr,
    fin,
    i_sem,
    w_sem,
    h_sem,
    ts_sem,
    tr_sem,
    tl_sem,
    ss_sem,
    sr_sem,
    ks_sem,
    kr_sem,
    ws_sem,
    wr_sem,
    gs_sem,
    gr_sem,
    xs_sem,
    xr_sem,
    fs_sem,
    fr_sem,
    fl_sem,
):
    me = lax.axis_index("dp")
    v = lax.axis_index("vocab")
    core = lax.rem(v, 2)
    sib_core = 1 - core
    sib = v + 1 - 2 * core
    across = lax.rem(v + 2, 4)
    slots, feat = hid_hbm.shape
    bal, vloc = teach_ref.shape
    steps = feat // KBLK
    rows = slots // GROUPS
    half = feat // 2
    chunks = half // CBLK
    per = rows // n
    dep = tin.shape[2]
    shift = n.bit_length() - 1

    small = [
        pltpu.make_async_copy(len_hbm, len_ref, i_sem.at[0]),
        pltpu.make_async_copy(soc_hbm, soc_ref, i_sem.at[1]),
        pltpu.make_async_copy(teach_hbm, teach_ref, i_sem.at[2]),
    ]
    for copy in small:
        copy.start()

    barrier = pltpu.get_barrier_semaphore()
    for k in range(1, n):
        pl.semaphore_signal(barrier, 1, device_id=(lax.rem(me + k, n), v), device_id_type=MESH)
    for k in range(1, nv):
        pl.semaphore_signal(barrier, 1, device_id=(me, lax.rem(v + k, nv)), device_id_type=MESH)

    def w_load(k):
        return pltpu.make_async_copy(
            w_hbm.at[pl.ds(pl.multiple_of(k * KBLK, KBLK), KBLK), :],
            w_v.at[pl.ds(pl.multiple_of(k * KBLK, KBLK), KBLK), :],
            w_sem.at[k],
        )

    def h_load(k):
        return pltpu.make_async_copy(
            hid_hbm.at[:, pl.ds(pl.multiple_of(k * KBLK, KBLK), KBLK)], h_v.at[k], h_sem.at[k]
        )

    @pl.loop(0, steps)
    def _(k):
        w_load(k).start()
        h_load(k).start()

    for copy in small:
        copy.wait()

    lens, offs, run = [], [], jnp.int32(0)
    for s in range(n):
        ln = len_ref[s]
        lens.append(ln)
        offs.append(run)
        run = run + ln
    zero = jnp.int32(0)
    inv_me, off_me, len_me = zero, zero, zero
    for s in range(n):
        inv_me = inv_me + jnp.where(soc_ref[s] == me, jnp.int32(s), zero)
        off_me = off_me + jnp.where(me == s, offs[s], zero)
        len_me = len_me + jnp.where(me == s, lens[s], zero)

    for g in range(GROUPS):
        for s in range(n):
            b0 = lax.shift_right_logical(offs[s] + ((inv_me - offs[s]) & (n - 1)), shift)
            first = b0 + g * per
            r = lax.broadcasted_iota(jnp.int32, (dep, bal), 0)
            b = lax.broadcasted_iota(jnp.int32, (dep, bal), 1)
            hot = jnp.where(b == r + first, 1.0, 0.0).astype(jnp.bfloat16)
            tout[g, s] = jnp.dot(
                hot, teach_ref[...], preferred_element_type=jnp.float32
            ).astype(jnp.bfloat16)

    def t_send(g, to):
        return pltpu.make_async_remote_copy(
            src_ref=tout.at[g, to],
            dst_ref=tin.at[g, me],
            send_sem=ts_sem.at[g, to],
            recv_sem=tr_sem.at[g, me],
            device_id=(to, v),
            device_id_type=MESH,
        )

    def t_recv(g, frm):
        return pltpu.make_async_remote_copy(
            src_ref=tout.at[g, frm],
            dst_ref=tin.at[g, frm],
            send_sem=ts_sem.at[g, frm],
            recv_sem=tr_sem.at[g, frm],
            device_id=(frm, v),
            device_id_type=MESH,
        )

    def t_own(g):
        return pltpu.make_async_copy(tout.at[g, me], tin.at[g, me], tl_sem.at[g])

    def w_push(j):
        row = pl.multiple_of(sib_core * half + j * CBLK, CBLK)
        return pltpu.make_async_remote_copy(
            src_ref=w_hbm.at[pl.ds(row, CBLK), :],
            dst_ref=w_sib.at[j],
            send_sem=ws_sem.at[j],
            recv_sem=wr_sem.at[j],
            device_id=(me, sib),
            device_id_type=MESH,
        )

    pl.semaphore_wait(barrier, n - 1 + nv - 1)
    for g in range(GROUPS):
        if g == 1:

            @pl.loop(0, chunks)
            def _(j):
                w_push(j).start()

        t_own(g).start()

        @pl.loop(1, n)
        def _(k):
            t_send(g, lax.rem(me + k, n)).start()

    z_v[...] = jnp.zeros_like(z_v)

    @pl.loop(0, steps)
    def _(k):
        w_load(k).wait()
        h_load(k).wait()
        z_v[...] += jnp.dot(
            h_v[k],
            w_v[pl.ds(pl.multiple_of(k * KBLK, KBLK), KBLK), :],
            preferred_element_type=jnp.float32,
        )

    def s_copy(g, frm, to):
        return pltpu.make_async_remote_copy(
            src_ref=st.at[g, frm],
            dst_ref=st.at[g, frm],
            send_sem=ss_sem.at[g, to],
            recv_sem=sr_sem.at[g, frm],
            device_id=(me, to),
            device_id_type=MESH,
        )

    def g_copy(g):
        return pltpu.make_async_remote_copy(
            src_ref=g_v.at[pl.ds(g * rows, rows), :],
            dst_ref=g_sib.at[pl.ds(g * rows, rows), :],
            send_sem=gs_sem.at[g],
            recv_sem=gr_sem.at[g],
            device_id=(me, sib),
            device_id_type=MESH,
        )

    def x_copy(g, j):
        return pltpu.make_async_remote_copy(
            src_ref=xs.at[g, j],
            dst_ref=xr.at[g, j],
            send_sem=xs_sem.at[g, j],
            recv_sem=xr_sem.at[g, j],
            device_id=(me, across),
            device_id_type=MESH,
        )

    def place(g, owner, j):
        col = pl.multiple_of(owner * half + j * CBLK, 128)
        return out_hbm.at[pl.ds(g * rows, rows), pl.ds(col, CBLK)]

    def f_send(g, j):
        return pltpu.make_async_remote_copy(
            src_ref=fin.at[g, j],
            dst_ref=place(g, core, j),
            send_sem=fs_sem.at[g, j],
            recv_sem=fr_sem.at[g, j],
            device_id=(me, sib),
            device_id_type=MESH,
        )

    def f_recv(g, j):
        return pltpu.make_async_remote_copy(
            src_ref=fin.at[g, j],
            dst_ref=place(g, 1 - core, j),
            send_sem=fs_sem.at[g, j],
            recv_sem=fr_sem.at[g, j],
            device_id=(me, sib),
            device_id_type=MESH,
        )

    def f_own(g, j):
        return pltpu.make_async_copy(fin.at[g, j], place(g, core, j), fl_sem.at[g, j])

    def back(grad, weight):
        return lax.dot_general(
            grad, weight, (((1,), (1,)), ((), ())), preferred_element_type=jnp.float32
        )

    for g in range(GROUPS):
        span = pl.ds(g * rows, rows)
        slot = lax.broadcasted_iota(jnp.int32, (rows, 1), 0) + g * rows
        live = slot < len_me
        cls = (off_me + slot) & (n - 1)
        owner = jnp.zeros((rows, 1), jnp.int32)
        for c in range(n):
            owner = owner + jnp.where(cls == c, soc_ref[c], zero)
        rank = lax.shift_right_logical(slot, shift) - g * per
        pick = owner * dep + rank
        lane = lax.broadcasted_iota(jnp.int32, (rows, n * dep), 1)
        hot = jnp.where(lane == pick, 1.0, 0.0).astype(jnp.bfloat16)

        t_own(g).wait()

        @pl.loop(1, n)
        def _(k):
            t_recv(g, lax.rem(me + k, n)).wait_recv()

        t = jnp.dot(
            hot, tin[g].reshape(n * dep, vloc), preferred_element_type=jnp.float32
        )
        z = jnp.where(live, z_v[span, :], 0.0)
        q = jnp.exp(t)
        q_v[span, :] = q
        top = jnp.max(z, axis=1, keepdims=True)
        total = jnp.sum(jnp.exp(z - top), axis=1, keepdims=True)
        mass = jnp.sum(q, axis=1, keepdims=True)
        cross = jnp.sum(q * (t - z), axis=1, keepdims=True)
        col = lax.broadcasted_iota(jnp.int32, (rows, 128), 1)
        packed = jnp.where(
            col == 0, top, jnp.where(col == 1, total, jnp.where(col == 2, mass, cross))
        )
        st[g, v] = packed.T[:8, :]

        @pl.loop(1, nv)
        def _(k):
            s_copy(g, v, lax.rem(v + k, nv)).start()

        @pl.loop(1, nv)
        def _(k):
            frm = lax.rem(v + k, nv)
            s_copy(g, frm, frm).wait_recv()

        peak = st[g, 0, 0:1, :]
        for u in range(1, nv):
            peak = jnp.maximum(peak, st[g, u, 0:1, :])
        sums = jnp.zeros_like(peak)
        masses = jnp.zeros_like(peak)
        crosses = jnp.zeros_like(peak)
        for u in range(nv):
            sums = sums + st[g, u, 1:2, :] * jnp.exp(st[g, u, 0:1, :] - peak)
            masses = masses + st[g, u, 2:3, :]
            crosses = crosses + st[g, u, 3:4, :]
        lse = peak + jnp.log(sums)
        klb[me, :, pl.ds(g * rows, rows)] = jnp.broadcast_to(crosses + masses * lse, (8, rows))
        sub = lax.broadcasted_iota(jnp.int32, (128, rows), 0)
        back_cols = jnp.where(sub == 0, lse, masses).T
        lse_c = back_cols[:, 0:1]
        mass_c = back_cols[:, 1:2]
        z = jnp.where(live, z_v[span, :], 0.0)
        grad = loss_scale * (mass_c * jnp.exp(z - lse_c) - q_v[span, :])
        g_v[span, :] = jnp.where(live, grad, 0.0).astype(jnp.bfloat16)

        g_copy(g).start()
        g_copy(g).wait_recv()

        @pl.loop(0, chunks)
        def _(j):
            if g == 0:
                w_push(j).wait_recv()
            own = w_v[pl.ds(pl.multiple_of(core * half + j * CBLK, CBLK), CBLK), :]
            mine = back(g_v[span, :], own) + back(g_sib[span, :], w_sib[j])
            xs[g, j] = mine.astype(jnp.bfloat16)
            x_copy(g, j).start()

    def k_copy(frm, to):
        return pltpu.make_async_remote_copy(
            src_ref=klb.at[frm],
            dst_ref=klb.at[frm],
            send_sem=ks_sem.at[to],
            recv_sem=kr_sem.at[frm],
            device_id=(to, v),
            device_id_type=MESH,
        )

    @pl.loop(1, n)
    def _(k):
        k_copy(me, lax.rem(me + k, n)).start()

    @pl.loop(1, n)
    def _(k):
        frm = lax.rem(me + k, n)
        k_copy(frm, frm).wait_recv()

    want = lax.broadcasted_iota(jnp.int32, (bal, slots), 0) * n + inv_me
    inner = lax.broadcasted_iota(jnp.int32, (bal, slots), 1)
    acc = jnp.zeros((bal, slots), jnp.float32)
    for s in range(n):
        hit = (want - offs[s] == inner) & (inner < lens[s])
        acc = jnp.where(hit, klb[s, 0:1, :], acc)
    kl_col = jnp.sum(acc, axis=1, keepdims=True)
    diag = lax.broadcasted_iota(jnp.int32, (bal, bal), 0) == lax.broadcasted_iota(
        jnp.int32, (bal, bal), 1
    )
    kl_ref[...] = jnp.sum(jnp.where(diag, kl_col, 0.0), axis=0, keepdims=True)

    for g in range(GROUPS):

        @pl.loop(0, chunks)
        def _(j):
            x_copy(g, j).wait_recv()
            fin[g, j] = (xs[g, j].astype(jnp.float32) + xr[g, j].astype(jnp.float32)).astype(
                jnp.bfloat16
            )
            f_send(g, j).start()
            f_own(g, j).start()

    for g in range(GROUPS):

        @pl.loop(1, n)
        def _(k):
            t_send(g, lax.rem(me + k, n)).wait_send()

        g_copy(g).wait_send()

        @pl.loop(1, nv)
        def _(k):
            s_copy(g, v, lax.rem(v + k, nv)).wait_send()

        @pl.loop(0, chunks)
        def _(j):
            if g == 0:
                w_push(j).wait_send()
            x_copy(g, j).wait_send()
            f_send(g, j).wait_send()
            f_own(g, j).wait()
            f_recv(g, j).wait_recv()

    @pl.loop(1, n)
    def _(k):
        k_copy(me, lax.rem(me + k, n)).wait_send()


def body(hidden_rows, plan_lengths, shard_of_class, head_weight, teacher_logprobs):
    n = lax.axis_size("dp")
    nv = lax.axis_size("vocab")
    slots, feat = hidden_rows.shape
    bal, vloc = teacher_logprobs.shape
    steps = feat // KBLK
    rows = slots // GROUPS
    chunks = feat // 2 // CBLK
    dep = max(16, rows // n)
    dma = pltpu.SemaphoreType.DMA
    bf, f32 = jnp.bfloat16, jnp.float32
    flops = 4 * slots * feat * vloc
    row_grad, row_kl = pl.pallas_call(
        functools.partial(kernel, n, nv),
        out_shape=(
            jax.ShapeDtypeStruct((slots, feat), bf),
            jax.ShapeDtypeStruct((1, bal), f32),
        ),
        in_specs=[
            pl.BlockSpec(memory_space=pltpu.HBM),
            pl.BlockSpec(memory_space=pltpu.HBM),
            pl.BlockSpec(memory_space=pltpu.HBM),
            pl.BlockSpec(memory_space=pltpu.HBM),
            pl.BlockSpec(memory_space=pltpu.HBM),
        ],
        out_specs=(
            pl.BlockSpec(memory_space=pl.ANY),
            pl.BlockSpec(memory_space=pltpu.VMEM),
        ),
        scratch_shapes=[
            pltpu.SMEM(plan_lengths.shape, jnp.int32),
            pltpu.SMEM(shard_of_class.shape, jnp.int32),
            pltpu.VMEM((bal, vloc), bf),
            pltpu.VMEM((feat, vloc), bf),
            pltpu.VMEM((chunks, CBLK, vloc), bf),
            pltpu.VMEM((steps, slots, KBLK), bf),
            pltpu.VMEM((slots, vloc), f32),
            pltpu.VMEM((slots, vloc), f32),
            pltpu.VMEM((slots, vloc), bf),
            pltpu.VMEM((GROUPS, n, dep, vloc), bf),
            pltpu.VMEM((GROUPS, n, dep, vloc), bf),
            pltpu.VMEM((GROUPS, nv, 8, rows), f32),
            pltpu.VMEM((n, 8, slots), f32),
            pltpu.VMEM((slots, vloc), bf),
            pltpu.VMEM((GROUPS, chunks, rows, CBLK), bf),
            pltpu.VMEM((GROUPS, chunks, rows, CBLK), bf),
            pltpu.VMEM((GROUPS, chunks, rows, CBLK), bf),
            dma((3,)),
            dma((steps,)),
            dma((steps,)),
            dma((GROUPS, n)),
            dma((GROUPS, n)),
            dma((GROUPS,)),
            dma((GROUPS, nv)),
            dma((GROUPS, nv)),
            dma((n,)),
            dma((n,)),
            dma((chunks,)),
            dma((chunks,)),
            dma((GROUPS,)),
            dma((GROUPS,)),
            dma((GROUPS, chunks)),
            dma((GROUPS, chunks)),
            dma((GROUPS, chunks)),
            dma((GROUPS, chunks)),
            dma((GROUPS, chunks)),
        ],
        compiler_params=pltpu.CompilerParams(
            collective_id=0, has_side_effects=True, vmem_limit_bytes=50 * 1024 * 1024
        ),
        cost_estimate=pl.CostEstimate(
            flops=flops, bytes_accessed=2 * feat * (vloc + 2 * slots), transcendentals=3 * slots * vloc
        ),
        name="plan_loss",
    )(plan_lengths, shard_of_class, teacher_logprobs, hidden_rows, head_weight)
    return row_grad, row_kl.reshape(bal)


def solution(mesh):
    return jax.shard_map(
        body,
        mesh=mesh,
        in_specs=(P("dp", None), P(), P(), P(None, "vocab"), P("dp", "vocab")),
        out_specs=(P("dp", None), P("dp")),
        check_vma=False,
    )
```

```python
import functools

import jax
import jax.numpy as jnp
from jax import lax
from jax.experimental import pallas as pl
from jax.experimental.pallas import tpu as pltpu
from jax.sharding import PartitionSpec as P

loss_scale = 64.0
MESH = pl.DeviceIdType.MESH
GROUPS = 2
KBLK = 512
CBLK = 256


def kernel(
    n,
    nv,
    len_hbm,
    soc_hbm,
    teach_hbm,
    hid_hbm,
    w_hbm,
    out_hbm,
    kl_ref,
    len_ref,
    soc_ref,
    teach_ref,
    w_v,
    w_sib,
    h_v,
    z_v,
    q_v,
    g_v,
    tout,
    tin,
    st,
    klb,
    g_sib,
    xs,
    xr,
    fin,
    i_sem,
    w_sem,
    h_sem,
    ts_sem,
    tr_sem,
    tl_sem,
    ss_sem,
    sr_sem,
    ks_sem,
    kr_sem,
    ws_sem,
    wr_sem,
    gs_sem,
    gr_sem,
    xs_sem,
    xr_sem,
    fs_sem,
    fr_sem,
    fl_sem,
):
    me = lax.axis_index("dp")
    v = lax.axis_index("vocab")
    core = lax.rem(v, 2)
    sib_core = 1 - core
    sib = v + 1 - 2 * core
    across = lax.rem(v + 2, 4)
    slots, feat = hid_hbm.shape
    bal, vloc = teach_ref.shape
    steps = feat // KBLK
    rows = slots // GROUPS
    half = feat // 2
    chunks = half // CBLK
    per = rows // n
    dep = tin.shape[2]
    shift = n.bit_length() - 1

    small = [
        pltpu.make_async_copy(len_hbm, len_ref, i_sem.at[0]),
        pltpu.make_async_copy(soc_hbm, soc_ref, i_sem.at[1]),
        pltpu.make_async_copy(teach_hbm, teach_ref, i_sem.at[2]),
    ]
    for copy in small:
        copy.start()

    barrier = pltpu.get_barrier_semaphore()
    for k in range(1, n):
        pl.semaphore_signal(barrier, 1, device_id=(lax.rem(me + k, n), v), device_id_type=MESH)
    for k in range(1, nv):
        pl.semaphore_signal(barrier, 1, device_id=(me, lax.rem(v + k, nv)), device_id_type=MESH)

    def w_load(k):
        return pltpu.make_async_copy(
            w_hbm.at[pl.ds(pl.multiple_of(k * KBLK, KBLK), KBLK), :],
            w_v.at[pl.ds(pl.multiple_of(k * KBLK, KBLK), KBLK), :],
            w_sem.at[k],
        )

    def h_load(k):
        return pltpu.make_async_copy(
            hid_hbm.at[:, pl.ds(pl.multiple_of(k * KBLK, KBLK), KBLK)], h_v.at[k], h_sem.at[k]
        )

    @pl.loop(0, steps)
    def _(k):
        w_load(k).start()
        h_load(k).start()

    for copy in small:
        copy.wait()

    lens, offs, run = [], [], jnp.int32(0)
    for s in range(n):
        ln = len_ref[s]
        lens.append(ln)
        offs.append(run)
        run = run + ln
    zero = jnp.int32(0)
    inv_me, off_me, len_me = zero, zero, zero
    for s in range(n):
        inv_me = inv_me + jnp.where(soc_ref[s] == me, jnp.int32(s), zero)
        off_me = off_me + jnp.where(me == s, offs[s], zero)
        len_me = len_me + jnp.where(me == s, lens[s], zero)

    line = lax.broadcasted_iota(jnp.int32, (n * dep, 1), 0)
    first = jnp.zeros((n * dep, 1), jnp.int32)
    for s in range(n):
        b0 = lax.shift_right_logical(offs[s] + ((inv_me - offs[s]) & (n - 1)), shift)
        inside = (line >= s * dep) & (line < (s + 1) * dep)
        first = jnp.where(inside, b0 - s * dep, first)
    target = line + first
    b = lax.broadcasted_iota(jnp.int32, (n * dep, bal), 1)
    for g in range(GROUPS):
        hot = jnp.where(b == target + g * per, 1.0, 0.0).astype(jnp.bfloat16)
        tout[g] = (
            jnp.dot(hot, teach_ref[...], preferred_element_type=jnp.float32)
            .astype(jnp.bfloat16)
            .reshape(n, dep, vloc)
        )

    def t_send(g, to):
        return pltpu.make_async_remote_copy(
            src_ref=tout.at[g, to],
            dst_ref=tin.at[g, me],
            send_sem=ts_sem.at[g, to],
            recv_sem=tr_sem.at[g, me],
            device_id=(to, v),
            device_id_type=MESH,
        )

    def t_recv(g, frm):
        return pltpu.make_async_remote_copy(
            src_ref=tout.at[g, frm],
            dst_ref=tin.at[g, frm],
            send_sem=ts_sem.at[g, frm],
            recv_sem=tr_sem.at[g, frm],
            device_id=(frm, v),
            device_id_type=MESH,
        )

    def t_own(g):
        return pltpu.make_async_copy(tout.at[g, me], tin.at[g, me], tl_sem.at[g])

    def w_push(j):
        row = pl.multiple_of(sib_core * half + j * CBLK, CBLK)
        return pltpu.make_async_remote_copy(
            src_ref=w_hbm.at[pl.ds(row, CBLK), :],
            dst_ref=w_sib.at[j],
            send_sem=ws_sem.at[j],
            recv_sem=wr_sem.at[j],
            device_id=(me, sib),
            device_id_type=MESH,
        )

    pl.semaphore_wait(barrier, n - 1 + nv - 1)
    for g in range(GROUPS):
        if g == 1:

            @pl.loop(0, chunks)
            def _(j):
                w_push(j).start()

        t_own(g).start()

        @pl.loop(1, n)
        def _(k):
            t_send(g, lax.rem(me + k, n)).start()

    z_v[...] = jnp.zeros_like(z_v)

    @pl.loop(0, steps)
    def _(k):
        w_load(k).wait()
        h_load(k).wait()
        z_v[...] += jnp.dot(
            h_v[k],
            w_v[pl.ds(pl.multiple_of(k * KBLK, KBLK), KBLK), :],
            preferred_element_type=jnp.float32,
        )

    def s_copy(g, frm, to):
        return pltpu.make_async_remote_copy(
            src_ref=st.at[g, frm],
            dst_ref=st.at[g, frm],
            send_sem=ss_sem.at[g, to],
            recv_sem=sr_sem.at[g, frm],
            device_id=(me, to),
            device_id_type=MESH,
        )

    def g_copy(g):
        return pltpu.make_async_remote_copy(
            src_ref=g_v.at[pl.ds(g * rows, rows), :],
            dst_ref=g_sib.at[pl.ds(g * rows, rows), :],
            send_sem=gs_sem.at[g],
            recv_sem=gr_sem.at[g],
            device_id=(me, sib),
            device_id_type=MESH,
        )

    def x_copy(g, j):
        return pltpu.make_async_remote_copy(
            src_ref=xs.at[g, j],
            dst_ref=xr.at[g, j],
            send_sem=xs_sem.at[g, j],
            recv_sem=xr_sem.at[g, j],
            device_id=(me, across),
            device_id_type=MESH,
        )

    def place(g, owner, j):
        col = pl.multiple_of(owner * half + j * CBLK, 128)
        return out_hbm.at[pl.ds(g * rows, rows), pl.ds(col, CBLK)]

    def f_send(g, j):
        return pltpu.make_async_remote_copy(
            src_ref=fin.at[g, j],
            dst_ref=place(g, core, j),
            send_sem=fs_sem.at[g, j],
            recv_sem=fr_sem.at[g, j],
            device_id=(me, sib),
            device_id_type=MESH,
        )

    def f_recv(g, j):
        return pltpu.make_async_remote_copy(
            src_ref=fin.at[g, j],
            dst_ref=place(g, 1 - core, j),
            send_sem=fs_sem.at[g, j],
            recv_sem=fr_sem.at[g, j],
            device_id=(me, sib),
            device_id_type=MESH,
        )

    def f_own(g, j):
        return pltpu.make_async_copy(fin.at[g, j], place(g, core, j), fl_sem.at[g, j])

    def back(grad, weight):
        return lax.dot_general(
            grad, weight, (((1,), (1,)), ((), ())), preferred_element_type=jnp.float32
        )

    for g in range(GROUPS):
        span = pl.ds(g * rows, rows)
        slot = lax.broadcasted_iota(jnp.int32, (rows, 1), 0) + g * rows
        live = slot < len_me
        cls = (off_me + slot) & (n - 1)
        owner = jnp.zeros((rows, 1), jnp.int32)
        for c in range(n):
            owner = owner + jnp.where(cls == c, soc_ref[c], zero)
        rank = lax.shift_right_logical(slot, shift) - g * per
        pick = owner * dep + rank
        lane = lax.broadcasted_iota(jnp.int32, (rows, n * dep), 1)
        hot = jnp.where(lane == pick, 1.0, 0.0).astype(jnp.bfloat16)

        t_own(g).wait()

        @pl.loop(1, n)
        def _(k):
            t_recv(g, lax.rem(me + k, n)).wait_recv()

        t = jnp.dot(
            hot, tin[g].reshape(n * dep, vloc), preferred_element_type=jnp.float32
        )
        z = jnp.where(live, z_v[span, :], 0.0)
        q = jnp.exp(t)
        q_v[span, :] = q
        top = jnp.max(z, axis=1, keepdims=True)
        total = jnp.sum(jnp.exp(z - top), axis=1, keepdims=True)
        mass = jnp.sum(q, axis=1, keepdims=True)
        cross = jnp.sum(q * (t - z), axis=1, keepdims=True)
        col = lax.broadcasted_iota(jnp.int32, (rows, 128), 1)
        packed = jnp.where(
            col == 0, top, jnp.where(col == 1, total, jnp.where(col == 2, mass, cross))
        )
        st[g, v] = packed.T[:8, :]

        @pl.loop(1, nv)
        def _(k):
            s_copy(g, v, lax.rem(v + k, nv)).start()

        @pl.loop(1, nv)
        def _(k):
            frm = lax.rem(v + k, nv)
            s_copy(g, frm, frm).wait_recv()

        peak = st[g, 0, 0:1, :]
        for u in range(1, nv):
            peak = jnp.maximum(peak, st[g, u, 0:1, :])
        sums = jnp.zeros_like(peak)
        masses = jnp.zeros_like(peak)
        crosses = jnp.zeros_like(peak)
        for u in range(nv):
            sums = sums + st[g, u, 1:2, :] * jnp.exp(st[g, u, 0:1, :] - peak)
            masses = masses + st[g, u, 2:3, :]
            crosses = crosses + st[g, u, 3:4, :]
        lse = peak + jnp.log(sums)
        klb[me, :, pl.ds(g * rows, rows)] = jnp.broadcast_to(crosses + masses * lse, (8, rows))
        sub = lax.broadcasted_iota(jnp.int32, (128, rows), 0)
        back_cols = jnp.where(sub == 0, lse, masses).T
        lse_c = back_cols[:, 0:1]
        mass_c = back_cols[:, 1:2]
        z = jnp.where(live, z_v[span, :], 0.0)
        grad = loss_scale * (mass_c * jnp.exp(z - lse_c) - q_v[span, :])
        g_v[span, :] = jnp.where(live, grad, 0.0).astype(jnp.bfloat16)

        g_copy(g).start()
        g_copy(g).wait_recv()

        @pl.loop(0, chunks)
        def _(j):
            if g == 0:
                w_push(j).wait_recv()
            own = w_v[pl.ds(pl.multiple_of(core * half + j * CBLK, CBLK), CBLK), :]
            mine = back(g_v[span, :], own) + back(g_sib[span, :], w_sib[j])
            xs[g, j] = mine.astype(jnp.bfloat16)
            x_copy(g, j).start()

    def k_copy(frm, to):
        return pltpu.make_async_remote_copy(
            src_ref=klb.at[frm],
            dst_ref=klb.at[frm],
            send_sem=ks_sem.at[to],
            recv_sem=kr_sem.at[frm],
            device_id=(to, v),
            device_id_type=MESH,
        )

    @pl.loop(1, n)
    def _(k):
        k_copy(me, lax.rem(me + k, n)).start()

    @pl.loop(1, n)
    def _(k):
        frm = lax.rem(me + k, n)
        k_copy(frm, frm).wait_recv()

    want = lax.broadcasted_iota(jnp.int32, (bal, slots), 0) * n + inv_me
    inner = lax.broadcasted_iota(jnp.int32, (bal, slots), 1)
    acc = jnp.zeros((bal, slots), jnp.float32)
    for s in range(n):
        hit = (want - offs[s] == inner) & (inner < lens[s])
        acc = jnp.where(hit, klb[s, 0:1, :], acc)
    kl_col = jnp.sum(acc, axis=1, keepdims=True)
    diag = lax.broadcasted_iota(jnp.int32, (bal, bal), 0) == lax.broadcasted_iota(
        jnp.int32, (bal, bal), 1
    )
    kl_ref[...] = jnp.sum(jnp.where(diag, kl_col, 0.0), axis=0, keepdims=True)

    for g in range(GROUPS):

        @pl.loop(0, chunks)
        def _(j):
            x_copy(g, j).wait_recv()
            fin[g, j] = (xs[g, j].astype(jnp.float32) + xr[g, j].astype(jnp.float32)).astype(
                jnp.bfloat16
            )
            f_send(g, j).start()
            f_own(g, j).start()

    for g in range(GROUPS):

        @pl.loop(1, n)
        def _(k):
            t_send(g, lax.rem(me + k, n)).wait_send()

        g_copy(g).wait_send()

        @pl.loop(1, nv)
        def _(k):
            s_copy(g, v, lax.rem(v + k, nv)).wait_send()

        @pl.loop(0, chunks)
        def _(j):
            if g == 0:
                w_push(j).wait_send()
            x_copy(g, j).wait_send()
            f_send(g, j).wait_send()
            f_own(g, j).wait()
            f_recv(g, j).wait_recv()

    @pl.loop(1, n)
    def _(k):
        k_copy(me, lax.rem(me + k, n)).wait_send()


def body(hidden_rows, plan_lengths, shard_of_class, head_weight, teacher_logprobs):
    n = lax.axis_size("dp")
    nv = lax.axis_size("vocab")
    slots, feat = hidden_rows.shape
    bal, vloc = teacher_logprobs.shape
    steps = feat // KBLK
    rows = slots // GROUPS
    chunks = feat // 2 // CBLK
    dep = max(16, rows // n)
    dma = pltpu.SemaphoreType.DMA
    bf, f32 = jnp.bfloat16, jnp.float32
    flops = 4 * slots * feat * vloc
    row_grad, row_kl = pl.pallas_call(
        functools.partial(kernel, n, nv),
        out_shape=(
            jax.ShapeDtypeStruct((slots, feat), bf),
            jax.ShapeDtypeStruct((1, bal), f32),
        ),
        in_specs=[
            pl.BlockSpec(memory_space=pltpu.HBM),
            pl.BlockSpec(memory_space=pltpu.HBM),
            pl.BlockSpec(memory_space=pltpu.HBM),
            pl.BlockSpec(memory_space=pltpu.HBM),
            pl.BlockSpec(memory_space=pltpu.HBM),
        ],
        out_specs=(
            pl.BlockSpec(memory_space=pl.ANY),
            pl.BlockSpec(memory_space=pltpu.VMEM),
        ),
        scratch_shapes=[
            pltpu.SMEM(plan_lengths.shape, jnp.int32),
            pltpu.SMEM(shard_of_class.shape, jnp.int32),
            pltpu.VMEM((bal, vloc), bf),
            pltpu.VMEM((feat, vloc), bf),
            pltpu.VMEM((chunks, CBLK, vloc), bf),
            pltpu.VMEM((steps, slots, KBLK), bf),
            pltpu.VMEM((slots, vloc), f32),
            pltpu.VMEM((slots, vloc), f32),
            pltpu.VMEM((slots, vloc), bf),
            pltpu.VMEM((GROUPS, n, dep, vloc), bf),
            pltpu.VMEM((GROUPS, n, dep, vloc), bf),
            pltpu.VMEM((GROUPS, nv, 8, rows), f32),
            pltpu.VMEM((n, 8, slots), f32),
            pltpu.VMEM((slots, vloc), bf),
            pltpu.VMEM((GROUPS, chunks, rows, CBLK), bf),
            pltpu.VMEM((GROUPS, chunks, rows, CBLK), bf),
            pltpu.VMEM((GROUPS, chunks, rows, CBLK), bf),
            dma((3,)),
            dma((steps,)),
            dma((steps,)),
            dma((GROUPS, n)),
            dma((GROUPS, n)),
            dma((GROUPS,)),
            dma((GROUPS, nv)),
            dma((GROUPS, nv)),
            dma((n,)),
            dma((n,)),
            dma((chunks,)),
            dma((chunks,)),
            dma((GROUPS,)),
            dma((GROUPS,)),
            dma((GROUPS, chunks)),
            dma((GROUPS, chunks)),
            dma((GROUPS, chunks)),
            dma((GROUPS, chunks)),
            dma((GROUPS, chunks)),
        ],
        compiler_params=pltpu.CompilerParams(
            collective_id=0, has_side_effects=True, vmem_limit_bytes=50 * 1024 * 1024
        ),
        cost_estimate=pl.CostEstimate(
            flops=flops, bytes_accessed=2 * feat * (vloc + 2 * slots), transcendentals=3 * slots * vloc
        ),
        name="plan_loss",
    )(plan_lengths, shard_of_class, teacher_logprobs, hidden_rows, head_weight)
    return row_grad, row_kl.reshape(bal)


def solution(mesh):
    return jax.shard_map(
        body,
        mesh=mesh,
        in_specs=(P("dp", None), P(), P(), P(None, "vocab"), P("dp", "vocab")),
        out_specs=(P("dp", None), P("dp")),
        check_vma=False,
    )
```

```python
import functools

import jax
import jax.numpy as jnp
from jax import lax
from jax.experimental import pallas as pl
from jax.experimental.pallas import tpu as pltpu
from jax.sharding import PartitionSpec as P

loss_scale = 64.0
MESH = pl.DeviceIdType.MESH
GROUPS = 2
KBLK = 512
CBLK = 512


def kernel(
    n,
    nv,
    len_hbm,
    soc_hbm,
    teach_hbm,
    hid_hbm,
    w_hbm,
    out_hbm,
    kl_ref,
    len_ref,
    soc_ref,
    teach_ref,
    w_v,
    w_sib,
    h_v,
    z_v,
    q_v,
    g_v,
    tout,
    tin,
    st,
    klb,
    g_sib,
    xs,
    xr,
    fin,
    i_sem,
    w_sem,
    h_sem,
    ts_sem,
    tr_sem,
    tl_sem,
    ss_sem,
    sr_sem,
    ks_sem,
    kr_sem,
    ws_sem,
    wr_sem,
    gs_sem,
    gr_sem,
    xs_sem,
    xr_sem,
    fs_sem,
    fr_sem,
    fl_sem,
):
    me = lax.axis_index("dp")
    v = lax.axis_index("vocab")
    core = lax.rem(v, 2)
    sib_core = 1 - core
    sib = v + 1 - 2 * core
    across = lax.rem(v + 2, 4)
    slots, feat = hid_hbm.shape
    bal, vloc = teach_ref.shape
    steps = feat // KBLK
    rows = slots // GROUPS
    half = feat // 2
    chunks = half // CBLK
    per = rows // n
    dep = tin.shape[2]
    shift = n.bit_length() - 1

    small = [
        pltpu.make_async_copy(len_hbm, len_ref, i_sem.at[0]),
        pltpu.make_async_copy(soc_hbm, soc_ref, i_sem.at[1]),
        pltpu.make_async_copy(teach_hbm, teach_ref, i_sem.at[2]),
    ]
    for copy in small:
        copy.start()

    barrier = pltpu.get_barrier_semaphore()
    for k in range(1, n):
        pl.semaphore_signal(barrier, 1, device_id=(lax.rem(me + k, n), v), device_id_type=MESH)
    for k in range(1, nv):
        pl.semaphore_signal(barrier, 1, device_id=(me, lax.rem(v + k, nv)), device_id_type=MESH)

    def w_load(k):
        return pltpu.make_async_copy(
            w_hbm.at[pl.ds(pl.multiple_of(k * KBLK, KBLK), KBLK), :],
            w_v.at[pl.ds(pl.multiple_of(k * KBLK, KBLK), KBLK), :],
            w_sem.at[k],
        )

    def h_load(k):
        return pltpu.make_async_copy(
            hid_hbm.at[:, pl.ds(pl.multiple_of(k * KBLK, KBLK), KBLK)], h_v.at[k], h_sem.at[k]
        )

    @pl.loop(0, steps)
    def _(k):
        w_load(k).start()
        h_load(k).start()

    for copy in small:
        copy.wait()

    lens, offs, run = [], [], jnp.int32(0)
    for s in range(n):
        ln = len_ref[s]
        lens.append(ln)
        offs.append(run)
        run = run + ln
    zero = jnp.int32(0)
    inv_me, off_me, len_me = zero, zero, zero
    for s in range(n):
        inv_me = inv_me + jnp.where(soc_ref[s] == me, jnp.int32(s), zero)
        off_me = off_me + jnp.where(me == s, offs[s], zero)
        len_me = len_me + jnp.where(me == s, lens[s], zero)

    line = lax.broadcasted_iota(jnp.int32, (n * dep, 1), 0)
    first = jnp.zeros((n * dep, 1), jnp.int32)
    for s in range(n):
        b0 = lax.shift_right_logical(offs[s] + ((inv_me - offs[s]) & (n - 1)), shift)
        inside = (line >= s * dep) & (line < (s + 1) * dep)
        first = jnp.where(inside, b0 - s * dep, first)
    target = line + first
    b = lax.broadcasted_iota(jnp.int32, (n * dep, bal), 1)
    for g in range(GROUPS):
        hot = jnp.where(b == target + g * per, 1.0, 0.0).astype(jnp.bfloat16)
        tout[g] = (
            jnp.dot(hot, teach_ref[...], preferred_element_type=jnp.float32)
            .astype(jnp.bfloat16)
            .reshape(n, dep, vloc)
        )

    def t_send(g, to):
        return pltpu.make_async_remote_copy(
            src_ref=tout.at[g, to],
            dst_ref=tin.at[g, me],
            send_sem=ts_sem.at[g, to],
            recv_sem=tr_sem.at[g, me],
            device_id=(to, v),
            device_id_type=MESH,
        )

    def t_recv(g, frm):
        return pltpu.make_async_remote_copy(
            src_ref=tout.at[g, frm],
            dst_ref=tin.at[g, frm],
            send_sem=ts_sem.at[g, frm],
            recv_sem=tr_sem.at[g, frm],
            device_id=(frm, v),
            device_id_type=MESH,
        )

    def t_own(g):
        return pltpu.make_async_copy(tout.at[g, me], tin.at[g, me], tl_sem.at[g])

    def w_push(j):
        row = pl.multiple_of(sib_core * half + j * CBLK, CBLK)
        return pltpu.make_async_remote_copy(
            src_ref=w_hbm.at[pl.ds(row, CBLK), :],
            dst_ref=w_sib.at[j],
            send_sem=ws_sem.at[j],
            recv_sem=wr_sem.at[j],
            device_id=(me, sib),
            device_id_type=MESH,
        )

    pl.semaphore_wait(barrier, n - 1 + nv - 1)
    for g in range(GROUPS):
        if g == 1:

            @pl.loop(0, chunks)
            def _(j):
                w_push(j).start()

        t_own(g).start()

        @pl.loop(1, n)
        def _(k):
            t_send(g, lax.rem(me + k, n)).start()

    z_v[...] = jnp.zeros_like(z_v)

    @pl.loop(0, steps)
    def _(k):
        w_load(k).wait()
        h_load(k).wait()
        z_v[...] += jnp.dot(
            h_v[k],
            w_v[pl.ds(pl.multiple_of(k * KBLK, KBLK), KBLK), :],
            preferred_element_type=jnp.float32,
        )

    def s_copy(g, frm, to):
        return pltpu.make_async_remote_copy(
            src_ref=st.at[g, frm],
            dst_ref=st.at[g, frm],
            send_sem=ss_sem.at[g, to],
            recv_sem=sr_sem.at[g, frm],
            device_id=(me, to),
            device_id_type=MESH,
        )

    def g_copy(g):
        return pltpu.make_async_remote_copy(
            src_ref=g_v.at[g],
            dst_ref=g_sib.at[g],
            send_sem=gs_sem.at[g],
            recv_sem=gr_sem.at[g],
            device_id=(me, sib),
            device_id_type=MESH,
        )

    def x_copy(g, j):
        return pltpu.make_async_remote_copy(
            src_ref=xs.at[g, j],
            dst_ref=xr.at[g, j],
            send_sem=xs_sem.at[g, j],
            recv_sem=xr_sem.at[g, j],
            device_id=(me, across),
            device_id_type=MESH,
        )

    def place(g, owner, j):
        col = pl.multiple_of(owner * half + j * CBLK, 128)
        return out_hbm.at[pl.ds(g * rows, rows), pl.ds(col, CBLK)]

    def f_send(g, j):
        return pltpu.make_async_remote_copy(
            src_ref=fin.at[g, j],
            dst_ref=place(g, core, j),
            send_sem=fs_sem.at[g, j],
            recv_sem=fr_sem.at[g, j],
            device_id=(me, sib),
            device_id_type=MESH,
        )

    def f_recv(g, j):
        return pltpu.make_async_remote_copy(
            src_ref=fin.at[g, j],
            dst_ref=place(g, 1 - core, j),
            send_sem=fs_sem.at[g, j],
            recv_sem=fr_sem.at[g, j],
            device_id=(me, sib),
            device_id_type=MESH,
        )

    def f_own(g, j):
        return pltpu.make_async_copy(fin.at[g, j], place(g, core, j), fl_sem.at[g, j])

    def back(weight, grad):
        return jnp.dot(weight, grad, preferred_element_type=jnp.float32)

    for g in range(GROUPS):
        span = pl.ds(g * rows, rows)
        slot = lax.broadcasted_iota(jnp.int32, (rows, 1), 0) + g * rows
        live = slot < len_me
        cls = (off_me + slot) & (n - 1)
        owner = jnp.zeros((rows, 1), jnp.int32)
        for c in range(n):
            owner = owner + jnp.where(cls == c, soc_ref[c], zero)
        rank = lax.shift_right_logical(slot, shift) - g * per
        pick = owner * dep + rank
        lane = lax.broadcasted_iota(jnp.int32, (rows, n * dep), 1)
        hot = jnp.where(lane == pick, 1.0, 0.0).astype(jnp.bfloat16)

        t_own(g).wait()

        @pl.loop(1, n)
        def _(k):
            t_recv(g, lax.rem(me + k, n)).wait_recv()

        t = jnp.dot(
            hot, tin[g].reshape(n * dep, vloc), preferred_element_type=jnp.float32
        )
        z = jnp.where(live, z_v[span, :], 0.0)
        q = jnp.exp(t)
        q_v[span, :] = q
        top = jnp.max(z, axis=1, keepdims=True)
        total = jnp.sum(jnp.exp(z - top), axis=1, keepdims=True)
        mass = jnp.sum(q, axis=1, keepdims=True)
        cross = jnp.sum(q * (t - z), axis=1, keepdims=True)
        col = lax.broadcasted_iota(jnp.int32, (rows, 128), 1)
        packed = jnp.where(
            col == 0, top, jnp.where(col == 1, total, jnp.where(col == 2, mass, cross))
        )
        st[g, v] = packed.T[:8, :]

        @pl.loop(1, nv)
        def _(k):
            s_copy(g, v, lax.rem(v + k, nv)).start()

        @pl.loop(1, nv)
        def _(k):
            frm = lax.rem(v + k, nv)
            s_copy(g, frm, frm).wait_recv()

        peak = st[g, 0, 0:1, :]
        for u in range(1, nv):
            peak = jnp.maximum(peak, st[g, u, 0:1, :])
        sums = jnp.zeros_like(peak)
        masses = jnp.zeros_like(peak)
        crosses = jnp.zeros_like(peak)
        for u in range(nv):
            sums = sums + st[g, u, 1:2, :] * jnp.exp(st[g, u, 0:1, :] - peak)
            masses = masses + st[g, u, 2:3, :]
            crosses = crosses + st[g, u, 3:4, :]
        lse = peak + jnp.log(sums)
        klb[me, :, pl.ds(g * rows, rows)] = jnp.broadcast_to(crosses + masses * lse, (8, rows))
        sub = lax.broadcasted_iota(jnp.int32, (128, rows), 0)
        back_cols = jnp.where(sub == 0, lse, masses).T
        lse_c = back_cols[:, 0:1]
        mass_c = back_cols[:, 1:2]
        z = jnp.where(live, z_v[span, :], 0.0)
        grad = loss_scale * (mass_c * jnp.exp(z - lse_c) - q_v[span, :])
        g_v[g] = jnp.where(live, grad, 0.0).T.astype(jnp.bfloat16)

        g_copy(g).start()
        g_copy(g).wait_recv()

        @pl.loop(0, chunks)
        def _(j):
            if g == 0:
                w_push(j).wait_recv()
            own = w_v[pl.ds(pl.multiple_of(core * half + j * CBLK, CBLK), CBLK), :]
            mine = back(own, g_v[g]) + back(w_sib[j], g_sib[g])
            xs[g, j] = mine.astype(jnp.bfloat16)
            x_copy(g, j).start()

    def k_copy(frm, to):
        return pltpu.make_async_remote_copy(
            src_ref=klb.at[frm],
            dst_ref=klb.at[frm],
            send_sem=ks_sem.at[to],
            recv_sem=kr_sem.at[frm],
            device_id=(to, v),
            device_id_type=MESH,
        )

    @pl.loop(1, n)
    def _(k):
        k_copy(me, lax.rem(me + k, n)).start()

    @pl.loop(1, n)
    def _(k):
        frm = lax.rem(me + k, n)
        k_copy(frm, frm).wait_recv()

    want = lax.broadcasted_iota(jnp.int32, (bal, slots), 0) * n + inv_me
    inner = lax.broadcasted_iota(jnp.int32, (bal, slots), 1)
    acc = jnp.zeros((bal, slots), jnp.float32)
    for s in range(n):
        hit = (want - offs[s] == inner) & (inner < lens[s])
        acc = jnp.where(hit, klb[s, 0:1, :], acc)
    kl_col = jnp.sum(acc, axis=1, keepdims=True)
    diag = lax.broadcasted_iota(jnp.int32, (bal, bal), 0) == lax.broadcasted_iota(
        jnp.int32, (bal, bal), 1
    )
    kl_ref[...] = jnp.sum(jnp.where(diag, kl_col, 0.0), axis=0, keepdims=True)

    for g in range(GROUPS):

        @pl.loop(0, chunks)
        def _(j):
            x_copy(g, j).wait_recv()
            both = xs[g, j].astype(jnp.float32) + xr[g, j].astype(jnp.float32)
            fin[g, j] = both.T.astype(jnp.bfloat16)
            f_send(g, j).start()
            f_own(g, j).start()

    for g in range(GROUPS):

        @pl.loop(1, n)
        def _(k):
            t_send(g, lax.rem(me + k, n)).wait_send()

        g_copy(g).wait_send()

        @pl.loop(1, nv)
        def _(k):
            s_copy(g, v, lax.rem(v + k, nv)).wait_send()

        @pl.loop(0, chunks)
        def _(j):
            if g == 0:
                w_push(j).wait_send()
            x_copy(g, j).wait_send()
            f_send(g, j).wait_send()
            f_own(g, j).wait()
            f_recv(g, j).wait_recv()

    @pl.loop(1, n)
    def _(k):
        k_copy(me, lax.rem(me + k, n)).wait_send()


def body(hidden_rows, plan_lengths, shard_of_class, head_weight, teacher_logprobs):
    n = lax.axis_size("dp")
    nv = lax.axis_size("vocab")
    slots, feat = hidden_rows.shape
    bal, vloc = teacher_logprobs.shape
    steps = feat // KBLK
    rows = slots // GROUPS
    chunks = feat // 2 // CBLK
    dep = max(16, rows // n)
    dma = pltpu.SemaphoreType.DMA
    bf, f32 = jnp.bfloat16, jnp.float32
    flops = 4 * slots * feat * vloc
    row_grad, row_kl = pl.pallas_call(
        functools.partial(kernel, n, nv),
        out_shape=(
            jax.ShapeDtypeStruct((slots, feat), bf),
            jax.ShapeDtypeStruct((1, bal), f32),
        ),
        in_specs=[
            pl.BlockSpec(memory_space=pltpu.HBM),
            pl.BlockSpec(memory_space=pltpu.HBM),
            pl.BlockSpec(memory_space=pltpu.HBM),
            pl.BlockSpec(memory_space=pltpu.HBM),
            pl.BlockSpec(memory_space=pltpu.HBM),
        ],
        out_specs=(
            pl.BlockSpec(memory_space=pl.ANY),
            pl.BlockSpec(memory_space=pltpu.VMEM),
        ),
        scratch_shapes=[
            pltpu.SMEM(plan_lengths.shape, jnp.int32),
            pltpu.SMEM(shard_of_class.shape, jnp.int32),
            pltpu.VMEM((bal, vloc), bf),
            pltpu.VMEM((feat, vloc), bf),
            pltpu.VMEM((chunks, CBLK, vloc), bf),
            pltpu.VMEM((steps, slots, KBLK), bf),
            pltpu.VMEM((slots, vloc), f32),
            pltpu.VMEM((slots, vloc), f32),
            pltpu.VMEM((GROUPS, vloc, rows), bf),
            pltpu.VMEM((GROUPS, n, dep, vloc), bf),
            pltpu.VMEM((GROUPS, n, dep, vloc), bf),
            pltpu.VMEM((GROUPS, nv, 8, rows), f32),
            pltpu.VMEM((n, 8, slots), f32),
            pltpu.VMEM((GROUPS, vloc, rows), bf),
            pltpu.VMEM((GROUPS, chunks, CBLK, rows), bf),
            pltpu.VMEM((GROUPS, chunks, CBLK, rows), bf),
            pltpu.VMEM((GROUPS, chunks, rows, CBLK), bf),
            dma((3,)),
            dma((steps,)),
            dma((steps,)),
            dma((GROUPS, n)),
            dma((GROUPS, n)),
            dma((GROUPS,)),
            dma((GROUPS, nv)),
            dma((GROUPS, nv)),
            dma((n,)),
            dma((n,)),
            dma((chunks,)),
            dma((chunks,)),
            dma((GROUPS,)),
            dma((GROUPS,)),
            dma((GROUPS, chunks)),
            dma((GROUPS, chunks)),
            dma((GROUPS, chunks)),
            dma((GROUPS, chunks)),
            dma((GROUPS, chunks)),
        ],
        compiler_params=pltpu.CompilerParams(
            collective_id=0, has_side_effects=True, vmem_limit_bytes=50 * 1024 * 1024
        ),
        cost_estimate=pl.CostEstimate(
            flops=flops, bytes_accessed=2 * feat * (vloc + 2 * slots), transcendentals=3 * slots * vloc
        ),
        name="plan_loss",
    )(plan_lengths, shard_of_class, teacher_logprobs, hidden_rows, head_weight)
    return row_grad, row_kl.reshape(bal)


def solution(mesh):
    return jax.shard_map(
        body,
        mesh=mesh,
        in_specs=(P("dp", None), P(), P(), P(None, "vocab"), P("dp", "vocab")),
        out_specs=(P("dp", None), P("dp")),
        check_vma=False,
    )
```

```python
import functools

import jax
import jax.numpy as jnp
from jax import lax
from jax.experimental import pallas as pl
from jax.experimental.pallas import tpu as pltpu
from jax.sharding import PartitionSpec as P

loss_scale = 64.0
MESH = pl.DeviceIdType.MESH
GROUPS = 2
KBLK = 512
CBLK = 512


def kernel(
    n,
    nv,
    len_hbm,
    soc_hbm,
    teach_hbm,
    hid_hbm,
    w_hbm,
    out_hbm,
    kl_ref,
    len_ref,
    soc_ref,
    teach_ref,
    w_v,
    w_sib,
    h_v,
    z_v,
    q_v,
    g_v,
    tout,
    tin,
    st,
    klb,
    g_sib,
    xs,
    xr,
    fin,
    i_sem,
    w_sem,
    h_sem,
    ts_sem,
    tr_sem,
    tl_sem,
    ss_sem,
    sr_sem,
    ks_sem,
    kr_sem,
    ws_sem,
    wr_sem,
    gs_sem,
    gr_sem,
    xs_sem,
    xr_sem,
    fs_sem,
    fr_sem,
    fl_sem,
):
    me = lax.axis_index("dp")
    v = lax.axis_index("vocab")
    core = lax.rem(v, 2)
    sib_core = 1 - core
    sib = v + 1 - 2 * core
    across = lax.rem(v + 2, 4)
    slots, feat = hid_hbm.shape
    bal, vloc = teach_ref.shape
    steps = feat // KBLK
    rows = slots // GROUPS
    half = feat // 2
    chunks = half // CBLK
    per = rows // n
    dep = tin.shape[2]
    shift = n.bit_length() - 1

    small = [
        pltpu.make_async_copy(len_hbm, len_ref, i_sem.at[0]),
        pltpu.make_async_copy(soc_hbm, soc_ref, i_sem.at[1]),
        pltpu.make_async_copy(teach_hbm, teach_ref, i_sem.at[2]),
    ]
    for copy in small:
        copy.start()

    barrier = pltpu.get_barrier_semaphore()
    for k in range(1, n):
        pl.semaphore_signal(barrier, 1, device_id=(lax.rem(me + k, n), v), device_id_type=MESH)
    for k in range(1, nv):
        pl.semaphore_signal(barrier, 1, device_id=(me, lax.rem(v + k, nv)), device_id_type=MESH)

    def w_load(k):
        return pltpu.make_async_copy(
            w_hbm.at[pl.ds(pl.multiple_of(k * KBLK, KBLK), KBLK), :],
            w_v.at[pl.ds(pl.multiple_of(k * KBLK, KBLK), KBLK), :],
            w_sem.at[k],
        )

    def h_load(k):
        return pltpu.make_async_copy(
            hid_hbm.at[:, pl.ds(pl.multiple_of(k * KBLK, KBLK), KBLK)], h_v.at[k], h_sem.at[k]
        )

    @pl.loop(0, steps)
    def _(k):
        w_load(k).start()
        h_load(k).start()

    for copy in small:
        copy.wait()

    lens, offs, run = [], [], jnp.int32(0)
    for s in range(n):
        ln = len_ref[s]
        lens.append(ln)
        offs.append(run)
        run = run + ln
    zero = jnp.int32(0)
    inv_me, off_me, len_me = zero, zero, zero
    for s in range(n):
        inv_me = inv_me + jnp.where(soc_ref[s] == me, jnp.int32(s), zero)
        off_me = off_me + jnp.where(me == s, offs[s], zero)
        len_me = len_me + jnp.where(me == s, lens[s], zero)

    line = lax.broadcasted_iota(jnp.int32, (n * dep, 1), 0)
    first = jnp.zeros((n * dep, 1), jnp.int32)
    for s in range(n):
        b0 = lax.shift_right_logical(offs[s] + ((inv_me - offs[s]) & (n - 1)), shift)
        inside = (line >= s * dep) & (line < (s + 1) * dep)
        first = jnp.where(inside, b0 - s * dep, first)
    target = line + first
    b = lax.broadcasted_iota(jnp.int32, (n * dep, bal), 1)
    for g in range(GROUPS):
        hot = jnp.where(b == target + g * per, 1.0, 0.0).astype(jnp.bfloat16)
        tout[g] = (
            jnp.dot(hot, teach_ref[...], preferred_element_type=jnp.float32)
            .astype(jnp.bfloat16)
            .reshape(n, dep, vloc)
        )

    def t_send(g, to):
        return pltpu.make_async_remote_copy(
            src_ref=tout.at[g, to],
            dst_ref=tin.at[g, me],
            send_sem=ts_sem.at[g, to],
            recv_sem=tr_sem.at[g, me],
            device_id=(to, v),
            device_id_type=MESH,
        )

    def t_recv(g, frm):
        return pltpu.make_async_remote_copy(
            src_ref=tout.at[g, frm],
            dst_ref=tin.at[g, frm],
            send_sem=ts_sem.at[g, frm],
            recv_sem=tr_sem.at[g, frm],
            device_id=(frm, v),
            device_id_type=MESH,
        )

    def t_own(g):
        return pltpu.make_async_copy(tout.at[g, me], tin.at[g, me], tl_sem.at[g])

    def w_push(j):
        row = pl.multiple_of(sib_core * half + j * CBLK, CBLK)
        return pltpu.make_async_remote_copy(
            src_ref=w_hbm.at[pl.ds(row, CBLK), :],
            dst_ref=w_sib.at[j],
            send_sem=ws_sem.at[j],
            recv_sem=wr_sem.at[j],
            device_id=(me, sib),
            device_id_type=MESH,
        )

    pl.semaphore_wait(barrier, n - 1 + nv - 1)
    for g in range(GROUPS):
        if g == 1:

            @pl.loop(0, chunks)
            def _(j):
                w_push(j).start()

        for k in sorted(range(1, n), key=lambda k: abs(2 * k - n)):
            t_send(g, lax.rem(me + k, n)).start()
        t_own(g).start()

    def s_copy(g, frm, to):
        return pltpu.make_async_remote_copy(
            src_ref=st.at[g, frm],
            dst_ref=st.at[g, frm],
            send_sem=ss_sem.at[g, to],
            recv_sem=sr_sem.at[g, frm],
            device_id=(me, to),
            device_id_type=MESH,
        )

    def g_copy(g):
        return pltpu.make_async_remote_copy(
            src_ref=g_v.at[g],
            dst_ref=g_sib.at[g],
            send_sem=gs_sem.at[g],
            recv_sem=gr_sem.at[g],
            device_id=(me, sib),
            device_id_type=MESH,
        )

    def x_copy(g, j):
        return pltpu.make_async_remote_copy(
            src_ref=xs.at[g, j],
            dst_ref=xr.at[g, j],
            send_sem=xs_sem.at[g, j],
            recv_sem=xr_sem.at[g, j],
            device_id=(me, across),
            device_id_type=MESH,
        )

    def place(g, owner, j):
        col = pl.multiple_of(owner * half + j * CBLK, 128)
        return out_hbm.at[pl.ds(g * rows, rows), pl.ds(col, CBLK)]

    def f_send(g, j):
        return pltpu.make_async_remote_copy(
            src_ref=fin.at[g, j],
            dst_ref=place(g, core, j),
            send_sem=fs_sem.at[g, j],
            recv_sem=fr_sem.at[g, j],
            device_id=(me, sib),
            device_id_type=MESH,
        )

    def f_recv(g, j):
        return pltpu.make_async_remote_copy(
            src_ref=fin.at[g, j],
            dst_ref=place(g, 1 - core, j),
            send_sem=fs_sem.at[g, j],
            recv_sem=fr_sem.at[g, j],
            device_id=(me, sib),
            device_id_type=MESH,
        )

    def f_own(g, j):
        return pltpu.make_async_copy(fin.at[g, j], place(g, core, j), fl_sem.at[g, j])

    def back(weight, grad):
        return jnp.dot(weight, grad, preferred_element_type=jnp.float32)

    for g in range(GROUPS):
        span = pl.ds(g * rows, rows)
        z_v[span, :] = jnp.zeros((rows, vloc), jnp.float32)

        @pl.loop(0, steps)
        def _(k):
            if g == 0:
                w_load(k).wait()
                h_load(k).wait()
            z_v[span, :] += jnp.dot(
                h_v[k, span, :],
                w_v[pl.ds(pl.multiple_of(k * KBLK, KBLK), KBLK), :],
                preferred_element_type=jnp.float32,
            )

        slot = lax.broadcasted_iota(jnp.int32, (rows, 1), 0) + g * rows
        live = slot < len_me
        cls = (off_me + slot) & (n - 1)
        owner = jnp.zeros((rows, 1), jnp.int32)
        for c in range(n):
            owner = owner + jnp.where(cls == c, soc_ref[c], zero)
        rank = lax.shift_right_logical(slot, shift) - g * per
        pick = owner * dep + rank
        lane = lax.broadcasted_iota(jnp.int32, (rows, n * dep), 1)
        hot = jnp.where(lane == pick, 1.0, 0.0).astype(jnp.bfloat16)

        t_own(g).wait()

        @pl.loop(1, n)
        def _(k):
            t_recv(g, lax.rem(me + k, n)).wait_recv()

        t = jnp.dot(
            hot, tin[g].reshape(n * dep, vloc), preferred_element_type=jnp.float32
        )
        z = jnp.where(live, z_v[span, :], 0.0)
        q = jnp.exp(t)
        q_v[span, :] = q
        top = jnp.max(z, axis=1, keepdims=True)
        total = jnp.sum(jnp.exp(z - top), axis=1, keepdims=True)
        mass = jnp.sum(q, axis=1, keepdims=True)
        cross = jnp.sum(q * (t - z), axis=1, keepdims=True)
        col = lax.broadcasted_iota(jnp.int32, (rows, 128), 1)
        packed = jnp.where(
            col == 0, top, jnp.where(col == 1, total, jnp.where(col == 2, mass, cross))
        )
        st[g, v] = packed.T[:8, :]

        @pl.loop(1, nv)
        def _(k):
            s_copy(g, v, lax.rem(v + k, nv)).start()

        @pl.loop(1, nv)
        def _(k):
            frm = lax.rem(v + k, nv)
            s_copy(g, frm, frm).wait_recv()

        peak = st[g, 0, 0:1, :]
        for u in range(1, nv):
            peak = jnp.maximum(peak, st[g, u, 0:1, :])
        sums = jnp.zeros_like(peak)
        masses = jnp.zeros_like(peak)
        crosses = jnp.zeros_like(peak)
        for u in range(nv):
            sums = sums + st[g, u, 1:2, :] * jnp.exp(st[g, u, 0:1, :] - peak)
            masses = masses + st[g, u, 2:3, :]
            crosses = crosses + st[g, u, 3:4, :]
        lse = peak + jnp.log(sums)
        klb[me, :, pl.ds(g * rows, rows)] = jnp.broadcast_to(crosses + masses * lse, (8, rows))
        sub = lax.broadcasted_iota(jnp.int32, (128, rows), 0)
        back_cols = jnp.where(sub == 0, lse, masses).T
        lse_c = back_cols[:, 0:1]
        mass_c = back_cols[:, 1:2]
        z = jnp.where(live, z_v[span, :], 0.0)
        grad = loss_scale * (mass_c * jnp.exp(z - lse_c) - q_v[span, :])
        g_v[g] = jnp.where(live, grad, 0.0).T.astype(jnp.bfloat16)

        g_copy(g).start()
        g_copy(g).wait_recv()

        @pl.loop(0, chunks)
        def _(j):
            if g == 0:
                w_push(j).wait_recv()
            own = w_v[pl.ds(pl.multiple_of(core * half + j * CBLK, CBLK), CBLK), :]
            mine = back(own, g_v[g]) + back(w_sib[j], g_sib[g])
            xs[g, j] = mine.astype(jnp.bfloat16)
            x_copy(g, j).start()

    def k_copy(frm, to):
        return pltpu.make_async_remote_copy(
            src_ref=klb.at[frm],
            dst_ref=klb.at[frm],
            send_sem=ks_sem.at[to],
            recv_sem=kr_sem.at[frm],
            device_id=(to, v),
            device_id_type=MESH,
        )

    @pl.loop(1, n)
    def _(k):
        k_copy(me, lax.rem(me + k, n)).start()

    def finish(g):
        @pl.loop(0, chunks)
        def _(j):
            x_copy(g, j).wait_recv()
            both = xs[g, j].astype(jnp.float32) + xr[g, j].astype(jnp.float32)
            fin[g, j] = both.T.astype(jnp.bfloat16)
            f_send(g, j).start()
            f_own(g, j).start()

    for g in range(GROUPS - 1):
        finish(g)

    @pl.loop(1, n)
    def _(k):
        frm = lax.rem(me + k, n)
        k_copy(frm, frm).wait_recv()

    want = lax.broadcasted_iota(jnp.int32, (bal, slots), 0) * n + inv_me
    inner = lax.broadcasted_iota(jnp.int32, (bal, slots), 1)
    acc = jnp.zeros((bal, slots), jnp.float32)
    for s in range(n):
        hit = (want - offs[s] == inner) & (inner < lens[s])
        acc = jnp.where(hit, klb[s, 0:1, :], acc)
    kl_col = jnp.sum(acc, axis=1, keepdims=True)
    diag = lax.broadcasted_iota(jnp.int32, (bal, bal), 0) == lax.broadcasted_iota(
        jnp.int32, (bal, bal), 1
    )
    kl_ref[...] = jnp.sum(jnp.where(diag, kl_col, 0.0), axis=0, keepdims=True)

    finish(GROUPS - 1)

    for g in range(GROUPS):

        @pl.loop(1, n)
        def _(k):
            t_send(g, lax.rem(me + k, n)).wait_send()

        g_copy(g).wait_send()

        @pl.loop(1, nv)
        def _(k):
            s_copy(g, v, lax.rem(v + k, nv)).wait_send()

        @pl.loop(0, chunks)
        def _(j):
            if g == 0:
                w_push(j).wait_send()
            x_copy(g, j).wait_send()
            f_send(g, j).wait_send()
            f_own(g, j).wait()
            f_recv(g, j).wait_recv()

    @pl.loop(1, n)
    def _(k):
        k_copy(me, lax.rem(me + k, n)).wait_send()


def body(hidden_rows, plan_lengths, shard_of_class, head_weight, teacher_logprobs):
    n = lax.axis_size("dp")
    nv = lax.axis_size("vocab")
    slots, feat = hidden_rows.shape
    bal, vloc = teacher_logprobs.shape
    steps = feat // KBLK
    rows = slots // GROUPS
    chunks = feat // 2 // CBLK
    dep = max(16, rows // n)
    dma = pltpu.SemaphoreType.DMA
    bf, f32 = jnp.bfloat16, jnp.float32
    flops = 4 * slots * feat * vloc
    row_grad, row_kl = pl.pallas_call(
        functools.partial(kernel, n, nv),
        out_shape=(
            jax.ShapeDtypeStruct((slots, feat), bf),
            jax.ShapeDtypeStruct((1, bal), f32),
        ),
        in_specs=[
            pl.BlockSpec(memory_space=pltpu.HBM),
            pl.BlockSpec(memory_space=pltpu.HBM),
            pl.BlockSpec(memory_space=pltpu.HBM),
            pl.BlockSpec(memory_space=pltpu.HBM),
            pl.BlockSpec(memory_space=pltpu.HBM),
        ],
        out_specs=(
            pl.BlockSpec(memory_space=pl.ANY),
            pl.BlockSpec(memory_space=pltpu.VMEM),
        ),
        scratch_shapes=[
            pltpu.SMEM(plan_lengths.shape, jnp.int32),
            pltpu.SMEM(shard_of_class.shape, jnp.int32),
            pltpu.VMEM((bal, vloc), bf),
            pltpu.VMEM((feat, vloc), bf),
            pltpu.VMEM((chunks, CBLK, vloc), bf),
            pltpu.VMEM((steps, slots, KBLK), bf),
            pltpu.VMEM((slots, vloc), f32),
            pltpu.VMEM((slots, vloc), f32),
            pltpu.VMEM((GROUPS, vloc, rows), bf),
            pltpu.VMEM((GROUPS, n, dep, vloc), bf),
            pltpu.VMEM((GROUPS, n, dep, vloc), bf),
            pltpu.VMEM((GROUPS, nv, 8, rows), f32),
            pltpu.VMEM((n, 8, slots), f32),
            pltpu.VMEM((GROUPS, vloc, rows), bf),
            pltpu.VMEM((GROUPS, chunks, CBLK, rows), bf),
            pltpu.VMEM((GROUPS, chunks, CBLK, rows), bf),
            pltpu.VMEM((GROUPS, chunks, rows, CBLK), bf),
            dma((3,)),
            dma((steps,)),
            dma((steps,)),
            dma((GROUPS, n)),
            dma((GROUPS, n)),
            dma((GROUPS,)),
            dma((GROUPS, nv)),
            dma((GROUPS, nv)),
            dma((n,)),
            dma((n,)),
            dma((chunks,)),
            dma((chunks,)),
            dma((GROUPS,)),
            dma((GROUPS,)),
            dma((GROUPS, chunks)),
            dma((GROUPS, chunks)),
            dma((GROUPS, chunks)),
            dma((GROUPS, chunks)),
            dma((GROUPS, chunks)),
        ],
        compiler_params=pltpu.CompilerParams(
            collective_id=0, has_side_effects=True, vmem_limit_bytes=50 * 1024 * 1024
        ),
        cost_estimate=pl.CostEstimate(
            flops=flops, bytes_accessed=2 * feat * (vloc + 2 * slots), transcendentals=3 * slots * vloc
        ),
        name="plan_loss",
    )(plan_lengths, shard_of_class, teacher_logprobs, hidden_rows, head_weight)
    return row_grad, row_kl.reshape(bal)


def solution(mesh):
    return jax.shard_map(
        body,
        mesh=mesh,
        in_specs=(P("dp", None), P(), P(), P(None, "vocab"), P("dp", "vocab")),
        out_specs=(P("dp", None), P("dp")),
        check_vma=False,
    )
```

```python
import functools

import jax
import jax.numpy as jnp
from jax import lax
from jax.experimental import pallas as pl
from jax.experimental.pallas import tpu as pltpu
from jax.sharding import PartitionSpec as P

loss_scale = 64.0
MESH = pl.DeviceIdType.MESH
GROUPS = 1
KBLK = 512
CBLK = 256


def kernel(
    n,
    nv,
    len_hbm,
    soc_hbm,
    teach_hbm,
    hid_hbm,
    w_hbm,
    out_hbm,
    kl_ref,
    len_ref,
    soc_ref,
    teach_ref,
    w_v,
    w_sib,
    h_v,
    z_v,
    q_v,
    g_v,
    tout,
    tin,
    st,
    klb,
    g_sib,
    xs,
    xr,
    fin,
    i_sem,
    w_sem,
    h_sem,
    ts_sem,
    tr_sem,
    tl_sem,
    ss_sem,
    sr_sem,
    ks_sem,
    kr_sem,
    ws_sem,
    wr_sem,
    gs_sem,
    gr_sem,
    xs_sem,
    xr_sem,
    fs_sem,
    fr_sem,
    fl_sem,
):
    me = lax.axis_index("dp")
    v = lax.axis_index("vocab")
    core = lax.rem(v, 2)
    sib_core = 1 - core
    sib = v + 1 - 2 * core
    across = lax.rem(v + 2, 4)
    slots, feat = hid_hbm.shape
    bal, vloc = teach_ref.shape
    steps = feat // KBLK
    rows = slots // GROUPS
    half = feat // 2
    chunks = half // CBLK
    per = rows // n
    dep = tin.shape[2]
    shift = n.bit_length() - 1

    small = [
        pltpu.make_async_copy(len_hbm, len_ref, i_sem.at[0]),
        pltpu.make_async_copy(soc_hbm, soc_ref, i_sem.at[1]),
        pltpu.make_async_copy(teach_hbm, teach_ref, i_sem.at[2]),
    ]
    for copy in small:
        copy.start()

    barrier = pltpu.get_barrier_semaphore()
    for k in range(1, n):
        pl.semaphore_signal(barrier, 1, device_id=(lax.rem(me + k, n), v), device_id_type=MESH)
    for k in range(1, nv):
        pl.semaphore_signal(barrier, 1, device_id=(me, lax.rem(v + k, nv)), device_id_type=MESH)

    def w_load(k):
        return pltpu.make_async_copy(
            w_hbm.at[pl.ds(pl.multiple_of(k * KBLK, KBLK), KBLK), :],
            w_v.at[pl.ds(pl.multiple_of(k * KBLK, KBLK), KBLK), :],
            w_sem.at[k],
        )

    def h_load(k):
        return pltpu.make_async_copy(
            hid_hbm.at[:, pl.ds(pl.multiple_of(k * KBLK, KBLK), KBLK)], h_v.at[k], h_sem.at[k]
        )

    @pl.loop(0, steps)
    def _(k):
        w_load(k).start()
        h_load(k).start()

    for copy in small:
        copy.wait()

    lens, offs, run = [], [], jnp.int32(0)
    for s in range(n):
        ln = len_ref[s]
        lens.append(ln)
        offs.append(run)
        run = run + ln
    zero = jnp.int32(0)
    inv_me, off_me, len_me = zero, zero, zero
    for s in range(n):
        inv_me = inv_me + jnp.where(soc_ref[s] == me, jnp.int32(s), zero)
        off_me = off_me + jnp.where(me == s, offs[s], zero)
        len_me = len_me + jnp.where(me == s, lens[s], zero)

    line = lax.broadcasted_iota(jnp.int32, (n * dep, 1), 0)
    first = jnp.zeros((n * dep, 1), jnp.int32)
    for s in range(n):
        b0 = lax.shift_right_logical(offs[s] + ((inv_me - offs[s]) & (n - 1)), shift)
        inside = (line >= s * dep) & (line < (s + 1) * dep)
        first = jnp.where(inside, b0 - s * dep, first)
    target = line + first
    b = lax.broadcasted_iota(jnp.int32, (n * dep, bal), 1)
    for g in range(GROUPS):
        hot = jnp.where(b == target + g * per, 1.0, 0.0).astype(jnp.bfloat16)
        tout[g] = (
            jnp.dot(hot, teach_ref[...], preferred_element_type=jnp.float32)
            .astype(jnp.bfloat16)
            .reshape(n, dep, vloc)
        )

    def t_send(g, to):
        return pltpu.make_async_remote_copy(
            src_ref=tout.at[g, to],
            dst_ref=tin.at[g, me],
            send_sem=ts_sem.at[g, to],
            recv_sem=tr_sem.at[g, me],
            device_id=(to, v),
            device_id_type=MESH,
        )

    def t_recv(g, frm):
        return pltpu.make_async_remote_copy(
            src_ref=tout.at[g, frm],
            dst_ref=tin.at[g, frm],
            send_sem=ts_sem.at[g, frm],
            recv_sem=tr_sem.at[g, frm],
            device_id=(frm, v),
            device_id_type=MESH,
        )

    def t_own(g):
        return pltpu.make_async_copy(tout.at[g, me], tin.at[g, me], tl_sem.at[g])

    def w_push(j):
        row = pl.multiple_of(sib_core * half + j * CBLK, CBLK)
        return pltpu.make_async_remote_copy(
            src_ref=w_hbm.at[pl.ds(row, CBLK), :],
            dst_ref=w_sib.at[j],
            send_sem=ws_sem.at[j],
            recv_sem=wr_sem.at[j],
            device_id=(me, sib),
            device_id_type=MESH,
        )

    pl.semaphore_wait(barrier, n - 1 + nv - 1)
    for g in range(GROUPS):
        for k in sorted(range(1, n), key=lambda k: abs(2 * k - n)):
            t_send(g, lax.rem(me + k, n)).start()
        t_own(g).start()
        if g == 0:

            @pl.loop(0, chunks)
            def _(j):
                w_push(j).start()

    def s_copy(g, frm, to):
        return pltpu.make_async_remote_copy(
            src_ref=st.at[g, frm],
            dst_ref=st.at[g, frm],
            send_sem=ss_sem.at[g, to],
            recv_sem=sr_sem.at[g, frm],
            device_id=(me, to),
            device_id_type=MESH,
        )

    def g_copy(g):
        return pltpu.make_async_remote_copy(
            src_ref=g_v.at[g],
            dst_ref=g_sib.at[g],
            send_sem=gs_sem.at[g],
            recv_sem=gr_sem.at[g],
            device_id=(me, sib),
            device_id_type=MESH,
        )

    def x_copy(g, j):
        return pltpu.make_async_remote_copy(
            src_ref=xs.at[g, j],
            dst_ref=xr.at[g, j],
            send_sem=xs_sem.at[g, j],
            recv_sem=xr_sem.at[g, j],
            device_id=(me, across),
            device_id_type=MESH,
        )

    def place(g, owner, j):
        col = pl.multiple_of(owner * half + j * CBLK, 128)
        return out_hbm.at[pl.ds(g * rows, rows), pl.ds(col, CBLK)]

    def f_send(g, j):
        return pltpu.make_async_remote_copy(
            src_ref=fin.at[g, j],
            dst_ref=place(g, core, j),
            send_sem=fs_sem.at[g, j],
            recv_sem=fr_sem.at[g, j],
            device_id=(me, sib),
            device_id_type=MESH,
        )

    def f_recv(g, j):
        return pltpu.make_async_remote_copy(
            src_ref=fin.at[g, j],
            dst_ref=place(g, 1 - core, j),
            send_sem=fs_sem.at[g, j],
            recv_sem=fr_sem.at[g, j],
            device_id=(me, sib),
            device_id_type=MESH,
        )

    def f_own(g, j):
        return pltpu.make_async_copy(fin.at[g, j], place(g, core, j), fl_sem.at[g, j])

    def back(weight, grad):
        return jnp.dot(weight, grad, preferred_element_type=jnp.float32)

    for g in range(GROUPS):
        span = pl.ds(g * rows, rows)
        z_v[span, :] = jnp.zeros((rows, vloc), jnp.float32)

        @pl.loop(0, steps)
        def _(k):
            if g == 0:
                w_load(k).wait()
                h_load(k).wait()
            z_v[span, :] += jnp.dot(
                h_v[k, span, :],
                w_v[pl.ds(pl.multiple_of(k * KBLK, KBLK), KBLK), :],
                preferred_element_type=jnp.float32,
            )

        slot = lax.broadcasted_iota(jnp.int32, (rows, 1), 0) + g * rows
        live = slot < len_me
        cls = (off_me + slot) & (n - 1)
        owner = jnp.zeros((rows, 1), jnp.int32)
        for c in range(n):
            owner = owner + jnp.where(cls == c, soc_ref[c], zero)
        rank = lax.shift_right_logical(slot, shift) - g * per
        pick = owner * dep + rank
        lane = lax.broadcasted_iota(jnp.int32, (rows, n * dep), 1)
        hot = jnp.where(lane == pick, 1.0, 0.0).astype(jnp.bfloat16)

        t_own(g).wait()

        @pl.loop(1, n)
        def _(k):
            t_recv(g, lax.rem(me + k, n)).wait_recv()

        t = jnp.dot(
            hot, tin[g].reshape(n * dep, vloc), preferred_element_type=jnp.float32
        )
        z = jnp.where(live, z_v[span, :], 0.0)
        q = jnp.exp(t)
        q_v[span, :] = q
        top = jnp.max(z, axis=1, keepdims=True)
        total = jnp.sum(jnp.exp(z - top), axis=1, keepdims=True)
        mass = jnp.sum(q, axis=1, keepdims=True)
        cross = jnp.sum(q * (t - z), axis=1, keepdims=True)
        col = lax.broadcasted_iota(jnp.int32, (rows, 128), 1)
        packed = jnp.where(
            col == 0, top, jnp.where(col == 1, total, jnp.where(col == 2, mass, cross))
        )
        st[g, v] = packed.T[:8, :]

        @pl.loop(1, nv)
        def _(k):
            s_copy(g, v, lax.rem(v + k, nv)).start()

        @pl.loop(1, nv)
        def _(k):
            frm = lax.rem(v + k, nv)
            s_copy(g, frm, frm).wait_recv()

        peak = st[g, 0, 0:1, :]
        for u in range(1, nv):
            peak = jnp.maximum(peak, st[g, u, 0:1, :])
        sums = jnp.zeros_like(peak)
        masses = jnp.zeros_like(peak)
        crosses = jnp.zeros_like(peak)
        for u in range(nv):
            sums = sums + st[g, u, 1:2, :] * jnp.exp(st[g, u, 0:1, :] - peak)
            masses = masses + st[g, u, 2:3, :]
            crosses = crosses + st[g, u, 3:4, :]
        lse = peak + jnp.log(sums)
        klb[me, :, pl.ds(g * rows, rows)] = jnp.broadcast_to(crosses + masses * lse, (8, rows))
        sub = lax.broadcasted_iota(jnp.int32, (128, rows), 0)
        back_cols = jnp.where(sub == 0, lse, masses).T
        lse_c = back_cols[:, 0:1]
        mass_c = back_cols[:, 1:2]
        z = jnp.where(live, z_v[span, :], 0.0)
        grad = loss_scale * (mass_c * jnp.exp(z - lse_c) - q_v[span, :])
        g_v[g] = jnp.where(live, grad, 0.0).T.astype(jnp.bfloat16)

        g_copy(g).start()
        g_copy(g).wait_recv()

        @pl.loop(0, chunks)
        def _(j):
            if g == 0:
                w_push(j).wait_recv()
            own = w_v[pl.ds(pl.multiple_of(core * half + j * CBLK, CBLK), CBLK), :]
            mine = back(own, g_v[g]) + back(w_sib[j], g_sib[g])
            xs[g, j] = mine.astype(jnp.bfloat16)
            x_copy(g, j).start()

    def k_copy(frm, to):
        return pltpu.make_async_remote_copy(
            src_ref=klb.at[frm],
            dst_ref=klb.at[frm],
            send_sem=ks_sem.at[to],
            recv_sem=kr_sem.at[frm],
            device_id=(to, v),
            device_id_type=MESH,
        )

    @pl.loop(1, n)
    def _(k):
        k_copy(me, lax.rem(me + k, n)).start()

    def finish(g):
        @pl.loop(0, chunks)
        def _(j):
            x_copy(g, j).wait_recv()
            both = xs[g, j].astype(jnp.float32) + xr[g, j].astype(jnp.float32)
            fin[g, j] = both.T.astype(jnp.bfloat16)
            f_send(g, j).start()
            f_own(g, j).start()

    for g in range(GROUPS - 1):
        finish(g)

    @pl.loop(1, n)
    def _(k):
        frm = lax.rem(me + k, n)
        k_copy(frm, frm).wait_recv()

    want = lax.broadcasted_iota(jnp.int32, (bal, slots), 0) * n + inv_me
    inner = lax.broadcasted_iota(jnp.int32, (bal, slots), 1)
    acc = jnp.zeros((bal, slots), jnp.float32)
    for s in range(n):
        hit = (want - offs[s] == inner) & (inner < lens[s])
        acc = jnp.where(hit, klb[s, 0:1, :], acc)
    kl_col = jnp.sum(acc, axis=1, keepdims=True)
    diag = lax.broadcasted_iota(jnp.int32, (bal, bal), 0) == lax.broadcasted_iota(
        jnp.int32, (bal, bal), 1
    )
    kl_ref[...] = jnp.sum(jnp.where(diag, kl_col, 0.0), axis=0, keepdims=True)

    finish(GROUPS - 1)

    for g in range(GROUPS):

        @pl.loop(1, n)
        def _(k):
            t_send(g, lax.rem(me + k, n)).wait_send()

        g_copy(g).wait_send()

        @pl.loop(1, nv)
        def _(k):
            s_copy(g, v, lax.rem(v + k, nv)).wait_send()

        @pl.loop(0, chunks)
        def _(j):
            if g == 0:
                w_push(j).wait_send()
            x_copy(g, j).wait_send()
            f_send(g, j).wait_send()
            f_own(g, j).wait()
            f_recv(g, j).wait_recv()

    @pl.loop(1, n)
    def _(k):
        k_copy(me, lax.rem(me + k, n)).wait_send()


def body(hidden_rows, plan_lengths, shard_of_class, head_weight, teacher_logprobs):
    n = lax.axis_size("dp")
    nv = lax.axis_size("vocab")
    slots, feat = hidden_rows.shape
    bal, vloc = teacher_logprobs.shape
    steps = feat // KBLK
    rows = slots // GROUPS
    chunks = feat // 2 // CBLK
    dep = max(16, rows // n)
    dma = pltpu.SemaphoreType.DMA
    bf, f32 = jnp.bfloat16, jnp.float32
    flops = 4 * slots * feat * vloc
    row_grad, row_kl = pl.pallas_call(
        functools.partial(kernel, n, nv),
        out_shape=(
            jax.ShapeDtypeStruct((slots, feat), bf),
            jax.ShapeDtypeStruct((1, bal), f32),
        ),
        in_specs=[
            pl.BlockSpec(memory_space=pltpu.HBM),
            pl.BlockSpec(memory_space=pltpu.HBM),
            pl.BlockSpec(memory_space=pltpu.HBM),
            pl.BlockSpec(memory_space=pltpu.HBM),
            pl.BlockSpec(memory_space=pltpu.HBM),
        ],
        out_specs=(
            pl.BlockSpec(memory_space=pl.ANY),
            pl.BlockSpec(memory_space=pltpu.VMEM),
        ),
        scratch_shapes=[
            pltpu.SMEM(plan_lengths.shape, jnp.int32),
            pltpu.SMEM(shard_of_class.shape, jnp.int32),
            pltpu.VMEM((bal, vloc), bf),
            pltpu.VMEM((feat, vloc), bf),
            pltpu.VMEM((chunks, CBLK, vloc), bf),
            pltpu.VMEM((steps, slots, KBLK), bf),
            pltpu.VMEM((slots, vloc), f32),
            pltpu.VMEM((slots, vloc), f32),
            pltpu.VMEM((GROUPS, vloc, rows), bf),
            pltpu.VMEM((GROUPS, n, dep, vloc), bf),
            pltpu.VMEM((GROUPS, n, dep, vloc), bf),
            pltpu.VMEM((GROUPS, nv, 8, rows), f32),
            pltpu.VMEM((n, 8, slots), f32),
            pltpu.VMEM((GROUPS, vloc, rows), bf),
            pltpu.VMEM((GROUPS, chunks, CBLK, rows), bf),
            pltpu.VMEM((GROUPS, chunks, CBLK, rows), bf),
            pltpu.VMEM((GROUPS, chunks, rows, CBLK), bf),
            dma((3,)),
            dma((steps,)),
            dma((steps,)),
            dma((GROUPS, n)),
            dma((GROUPS, n)),
            dma((GROUPS,)),
            dma((GROUPS, nv)),
            dma((GROUPS, nv)),
            dma((n,)),
            dma((n,)),
            dma((chunks,)),
            dma((chunks,)),
            dma((GROUPS,)),
            dma((GROUPS,)),
            dma((GROUPS, chunks)),
            dma((GROUPS, chunks)),
            dma((GROUPS, chunks)),
            dma((GROUPS, chunks)),
            dma((GROUPS, chunks)),
        ],
        compiler_params=pltpu.CompilerParams(
            collective_id=0, has_side_effects=True, vmem_limit_bytes=50 * 1024 * 1024
        ),
        cost_estimate=pl.CostEstimate(
            flops=flops, bytes_accessed=2 * feat * (vloc + 2 * slots), transcendentals=3 * slots * vloc
        ),
        name="plan_loss",
    )(plan_lengths, shard_of_class, teacher_logprobs, hidden_rows, head_weight)
    return row_grad, row_kl.reshape(bal)


def solution(mesh):
    return jax.shard_map(
        body,
        mesh=mesh,
        in_specs=(P("dp", None), P(), P(), P(None, "vocab"), P("dp", "vocab")),
        out_specs=(P("dp", None), P("dp")),
        check_vma=False,
    )
```

```python
import functools

import jax
import jax.numpy as jnp
from jax import lax
from jax.experimental import pallas as pl
from jax.experimental.pallas import tpu as pltpu
from jax.sharding import PartitionSpec as P

loss_scale = 64.0
MESH = pl.DeviceIdType.MESH
GROUPS = 1
KBLK = 512
CBLK = 256


def kernel(
    n,
    nv,
    len_hbm,
    soc_hbm,
    teach_hbm,
    hid_hbm,
    w_hbm,
    out_hbm,
    kl_ref,
    len_ref,
    soc_ref,
    teach_ref,
    w_v,
    w_sib,
    h_v,
    z_v,
    q_v,
    g_v,
    tout,
    tin,
    st,
    klb,
    g_sib,
    xs,
    xr,
    fin,
    i_sem,
    w_sem,
    h_sem,
    ts_sem,
    tr_sem,
    tl_sem,
    ss_sem,
    sr_sem,
    ks_sem,
    kr_sem,
    ws_sem,
    wr_sem,
    gs_sem,
    gr_sem,
    xs_sem,
    xr_sem,
    fs_sem,
    fr_sem,
    fl_sem,
):
    me = lax.axis_index("dp")
    v = lax.axis_index("vocab")
    core = lax.rem(v, 2)
    sib_core = 1 - core
    sib = v + 1 - 2 * core
    across = lax.rem(v + 2, 4)
    slots, feat = hid_hbm.shape
    bal, vloc = teach_ref.shape
    steps = feat // KBLK
    rows = slots // GROUPS
    half = feat // 2
    chunks = half // CBLK
    per = rows // n
    dep = tin.shape[2]
    shift = n.bit_length() - 1

    small = [
        pltpu.make_async_copy(len_hbm, len_ref, i_sem.at[0]),
        pltpu.make_async_copy(soc_hbm, soc_ref, i_sem.at[1]),
        pltpu.make_async_copy(teach_hbm, teach_ref, i_sem.at[2]),
    ]
    for copy in small:
        copy.start()

    barrier = pltpu.get_barrier_semaphore()
    for k in range(1, n):
        pl.semaphore_signal(barrier, 1, device_id=(lax.rem(me + k, n), v), device_id_type=MESH)
    for k in range(1, nv):
        pl.semaphore_signal(barrier, 1, device_id=(me, lax.rem(v + k, nv)), device_id_type=MESH)

    def w_load(k):
        return pltpu.make_async_copy(
            w_hbm.at[pl.ds(pl.multiple_of(k * KBLK, KBLK), KBLK), :],
            w_v.at[pl.ds(pl.multiple_of(k * KBLK, KBLK), KBLK), :],
            w_sem.at[k],
        )

    def h_load(k):
        return pltpu.make_async_copy(
            hid_hbm.at[:, pl.ds(pl.multiple_of(k * KBLK, KBLK), KBLK)], h_v.at[k], h_sem.at[k]
        )

    @pl.loop(0, steps)
    def _(k):
        w_load(k).start()
        h_load(k).start()

    for copy in small:
        copy.wait()

    lens, offs, run = [], [], jnp.int32(0)
    for s in range(n):
        ln = len_ref[s]
        lens.append(ln)
        offs.append(run)
        run = run + ln
    zero = jnp.int32(0)
    inv_me, off_me, len_me = zero, zero, zero
    for s in range(n):
        inv_me = inv_me + jnp.where(soc_ref[s] == me, jnp.int32(s), zero)
        off_me = off_me + jnp.where(me == s, offs[s], zero)
        len_me = len_me + jnp.where(me == s, lens[s], zero)

    line = lax.broadcasted_iota(jnp.int32, (n * dep, 1), 0)
    first = jnp.zeros((n * dep, 1), jnp.int32)
    for s in range(n):
        b0 = lax.shift_right_logical(offs[s] + ((inv_me - offs[s]) & (n - 1)), shift)
        inside = (line >= s * dep) & (line < (s + 1) * dep)
        first = jnp.where(inside, b0 - s * dep, first)
    target = line + first
    b = lax.broadcasted_iota(jnp.int32, (n * dep, bal), 1)
    for g in range(GROUPS):
        hot = jnp.where(b == target + g * per, 1.0, 0.0).astype(jnp.bfloat16)
        tout[g] = (
            jnp.dot(hot, teach_ref[...], preferred_element_type=jnp.float32)
            .astype(jnp.bfloat16)
            .reshape(n, dep, vloc)
        )

    def t_send(g, to):
        return pltpu.make_async_remote_copy(
            src_ref=tout.at[g, to],
            dst_ref=tin.at[g, me],
            send_sem=ts_sem.at[g, to],
            recv_sem=tr_sem.at[g, me],
            device_id=(to, v),
            device_id_type=MESH,
        )

    def t_recv(g, frm):
        return pltpu.make_async_remote_copy(
            src_ref=tout.at[g, frm],
            dst_ref=tin.at[g, frm],
            send_sem=ts_sem.at[g, frm],
            recv_sem=tr_sem.at[g, frm],
            device_id=(frm, v),
            device_id_type=MESH,
        )

    def t_own(g):
        return pltpu.make_async_copy(tout.at[g, me], tin.at[g, me], tl_sem.at[g])

    def w_push(j):
        row = pl.multiple_of(sib_core * half + j * CBLK, CBLK)
        return pltpu.make_async_remote_copy(
            src_ref=w_hbm.at[pl.ds(row, CBLK), :],
            dst_ref=w_sib.at[j],
            send_sem=ws_sem.at[j],
            recv_sem=wr_sem.at[j],
            device_id=(me, sib),
            device_id_type=MESH,
        )

    pl.semaphore_wait(barrier, n - 1 + nv - 1)
    for g in range(GROUPS):
        for k in sorted(range(1, n), key=lambda k: abs(2 * k - n)):
            t_send(g, lax.rem(me + k, n)).start()
        t_own(g).start()
        if g == 0:

            @pl.loop(0, chunks)
            def _(j):
                w_push(j).start()

    def s_copy(g, frm, to):
        return pltpu.make_async_remote_copy(
            src_ref=st.at[g, frm],
            dst_ref=st.at[g, frm],
            send_sem=ss_sem.at[g, to],
            recv_sem=sr_sem.at[g, frm],
            device_id=(me, to),
            device_id_type=MESH,
        )

    def g_copy(g):
        return pltpu.make_async_remote_copy(
            src_ref=g_v.at[g],
            dst_ref=g_sib.at[g],
            send_sem=gs_sem.at[g],
            recv_sem=gr_sem.at[g],
            device_id=(me, sib),
            device_id_type=MESH,
        )

    def x_copy(g, j):
        return pltpu.make_async_remote_copy(
            src_ref=xs.at[g, j],
            dst_ref=xr.at[g, j],
            send_sem=xs_sem.at[g, j],
            recv_sem=xr_sem.at[g, j],
            device_id=(me, across),
            device_id_type=MESH,
        )

    def place(g, owner, j):
        col = pl.multiple_of(owner * half + j * CBLK, 128)
        return out_hbm.at[pl.ds(g * rows, rows), pl.ds(col, CBLK)]

    def f_send(g, j):
        return pltpu.make_async_remote_copy(
            src_ref=fin.at[g, j],
            dst_ref=place(g, core, j),
            send_sem=fs_sem.at[g, j],
            recv_sem=fr_sem.at[g, j],
            device_id=(me, sib),
            device_id_type=MESH,
        )

    def f_recv(g, j):
        return pltpu.make_async_remote_copy(
            src_ref=fin.at[g, j],
            dst_ref=place(g, 1 - core, j),
            send_sem=fs_sem.at[g, j],
            recv_sem=fr_sem.at[g, j],
            device_id=(me, sib),
            device_id_type=MESH,
        )

    def f_own(g, j):
        return pltpu.make_async_copy(fin.at[g, j], place(g, core, j), fl_sem.at[g, j])

    def back(weight, grad):
        return jnp.dot(weight, grad, preferred_element_type=jnp.float32)

    for g in range(GROUPS):
        span = pl.ds(g * rows, rows)
        z_v[span, :] = jnp.zeros((rows, vloc), jnp.float32)

        @pl.loop(0, steps)
        def _(k):
            if g == 0:
                w_load(k).wait()
                h_load(k).wait()
            z_v[span, :] += jnp.dot(
                h_v[k, span, :],
                w_v[pl.ds(pl.multiple_of(k * KBLK, KBLK), KBLK), :],
                preferred_element_type=jnp.float32,
            )

        slot = lax.broadcasted_iota(jnp.int32, (rows, 1), 0) + g * rows
        live = slot < len_me
        cls = (off_me + slot) & (n - 1)
        owner = jnp.zeros((rows, 1), jnp.int32)
        for c in range(n):
            owner = owner + jnp.where(cls == c, soc_ref[c], zero)
        rank = lax.shift_right_logical(slot, shift) - g * per
        pick = owner * dep + rank
        lane = lax.broadcasted_iota(jnp.int32, (rows, n * dep), 1)
        hot = jnp.where(lane == pick, 1.0, 0.0).astype(jnp.bfloat16)

        t_own(g).wait()

        @pl.loop(1, n)
        def _(k):
            t_recv(g, lax.rem(me + k, n)).wait_recv()

        t = jnp.dot(
            hot, tin[g].reshape(n * dep, vloc), preferred_element_type=jnp.float32
        )
        z = jnp.where(live, z_v[span, :], 0.0)
        q = jnp.exp(t)
        q_v[span, :] = q
        top = jnp.max(z, axis=1, keepdims=True)
        total = jnp.sum(jnp.exp(z - top), axis=1, keepdims=True)
        mass = jnp.sum(q, axis=1, keepdims=True)
        cross = jnp.sum(q * (t - z), axis=1, keepdims=True)
        col = lax.broadcasted_iota(jnp.int32, (rows, 128), 1)
        packed = jnp.where(
            col == 0, top, jnp.where(col == 1, total, jnp.where(col == 2, mass, cross))
        )
        st[g, v] = packed.T[:8, :]

        @pl.loop(1, nv)
        def _(k):
            s_copy(g, v, lax.rem(v + k, nv)).start()

        @pl.loop(1, nv)
        def _(k):
            frm = lax.rem(v + k, nv)
            s_copy(g, frm, frm).wait_recv()

        peak = st[g, 0, 0:1, :]
        for u in range(1, nv):
            peak = jnp.maximum(peak, st[g, u, 0:1, :])
        sums = jnp.zeros_like(peak)
        masses = jnp.zeros_like(peak)
        crosses = jnp.zeros_like(peak)
        for u in range(nv):
            sums = sums + st[g, u, 1:2, :] * jnp.exp(st[g, u, 0:1, :] - peak)
            masses = masses + st[g, u, 2:3, :]
            crosses = crosses + st[g, u, 3:4, :]
        lse = peak + jnp.log(sums)
        klb[me, :, pl.ds(g * rows, rows)] = jnp.broadcast_to(crosses + masses * lse, (8, rows))
        sub = lax.broadcasted_iota(jnp.int32, (128, rows), 0)
        back_cols = jnp.where(sub == 0, lse, masses).T
        lse_c = back_cols[:, 0:1]
        mass_c = back_cols[:, 1:2]
        z = jnp.where(live, z_v[span, :], 0.0)
        grad = loss_scale * (mass_c * jnp.exp(z - lse_c) - q_v[span, :])
        g_v[g] = jnp.where(live, grad, 0.0).T.astype(jnp.bfloat16)

        g_copy(g).start()
        g_copy(g).wait_recv()

        @pl.loop(0, chunks)
        def _(j):
            if g == 0:
                w_push(j).wait_recv()
            own = w_v[pl.ds(pl.multiple_of(core * half + j * CBLK, CBLK), CBLK), :]
            mine = back(own, g_v[g]) + back(w_sib[j], g_sib[g])
            xs[g, j] = mine.astype(jnp.bfloat16)
            x_copy(g, j).start()

    def k_copy(frm, to):
        return pltpu.make_async_remote_copy(
            src_ref=klb.at[frm],
            dst_ref=klb.at[frm],
            send_sem=ks_sem.at[to],
            recv_sem=kr_sem.at[frm],
            device_id=(to, v),
            device_id_type=MESH,
        )

    @pl.loop(1, n)
    def _(k):
        k_copy(me, lax.rem(me + k, n)).start()

    def finish(g):
        @pl.loop(0, chunks)
        def _(j):
            x_copy(g, j).wait_recv()
            both = xs[g, j].astype(jnp.float32) + xr[g, j].astype(jnp.float32)
            fin[g, j] = both.T.astype(jnp.bfloat16)
            f_send(g, j).start()
            f_own(g, j).start()

    for g in range(GROUPS):
        finish(g)

    @pl.loop(1, n)
    def _(k):
        frm = lax.rem(me + k, n)
        k_copy(frm, frm).wait_recv()

    want = lax.broadcasted_iota(jnp.int32, (bal, slots), 0) * n + inv_me
    inner = lax.broadcasted_iota(jnp.int32, (bal, slots), 1)
    acc = jnp.zeros((bal, slots), jnp.float32)
    for s in range(n):
        hit = (want - offs[s] == inner) & (inner < lens[s])
        acc = jnp.where(hit, klb[s, 0:1, :], acc)
    kl_col = jnp.sum(acc, axis=1, keepdims=True)
    diag = lax.broadcasted_iota(jnp.int32, (bal, bal), 0) == lax.broadcasted_iota(
        jnp.int32, (bal, bal), 1
    )
    kl_ref[...] = jnp.sum(jnp.where(diag, kl_col, 0.0), axis=0, keepdims=True)

    for g in range(GROUPS):

        @pl.loop(1, n)
        def _(k):
            t_send(g, lax.rem(me + k, n)).wait_send()

        g_copy(g).wait_send()

        @pl.loop(1, nv)
        def _(k):
            s_copy(g, v, lax.rem(v + k, nv)).wait_send()

        @pl.loop(0, chunks)
        def _(j):
            if g == 0:
                w_push(j).wait_send()
            x_copy(g, j).wait_send()
            f_send(g, j).wait_send()
            f_own(g, j).wait()
            f_recv(g, j).wait_recv()

    @pl.loop(1, n)
    def _(k):
        k_copy(me, lax.rem(me + k, n)).wait_send()


def body(hidden_rows, plan_lengths, shard_of_class, head_weight, teacher_logprobs):
    n = lax.axis_size("dp")
    nv = lax.axis_size("vocab")
    slots, feat = hidden_rows.shape
    bal, vloc = teacher_logprobs.shape
    steps = feat // KBLK
    rows = slots // GROUPS
    chunks = feat // 2 // CBLK
    dep = max(16, rows // n)
    dma = pltpu.SemaphoreType.DMA
    bf, f32 = jnp.bfloat16, jnp.float32
    flops = 4 * slots * feat * vloc
    row_grad, row_kl = pl.pallas_call(
        functools.partial(kernel, n, nv),
        out_shape=(
            jax.ShapeDtypeStruct((slots, feat), bf),
            jax.ShapeDtypeStruct((1, bal), f32),
        ),
        in_specs=[
            pl.BlockSpec(memory_space=pltpu.HBM),
            pl.BlockSpec(memory_space=pltpu.HBM),
            pl.BlockSpec(memory_space=pltpu.HBM),
            pl.BlockSpec(memory_space=pltpu.HBM),
            pl.BlockSpec(memory_space=pltpu.HBM),
        ],
        out_specs=(
            pl.BlockSpec(memory_space=pl.ANY),
            pl.BlockSpec(memory_space=pltpu.VMEM),
        ),
        scratch_shapes=[
            pltpu.SMEM(plan_lengths.shape, jnp.int32),
            pltpu.SMEM(shard_of_class.shape, jnp.int32),
            pltpu.VMEM((bal, vloc), bf),
            pltpu.VMEM((feat, vloc), bf),
            pltpu.VMEM((chunks, CBLK, vloc), bf),
            pltpu.VMEM((steps, slots, KBLK), bf),
            pltpu.VMEM((slots, vloc), f32),
            pltpu.VMEM((slots, vloc), f32),
            pltpu.VMEM((GROUPS, vloc, rows), bf),
            pltpu.VMEM((GROUPS, n, dep, vloc), bf),
            pltpu.VMEM((GROUPS, n, dep, vloc), bf),
            pltpu.VMEM((GROUPS, nv, 8, rows), f32),
            pltpu.VMEM((n, 8, slots), f32),
            pltpu.VMEM((GROUPS, vloc, rows), bf),
            pltpu.VMEM((GROUPS, chunks, CBLK, rows), bf),
            pltpu.VMEM((GROUPS, chunks, CBLK, rows), bf),
            pltpu.VMEM((GROUPS, chunks, rows, CBLK), bf),
            dma((3,)),
            dma((steps,)),
            dma((steps,)),
            dma((GROUPS, n)),
            dma((GROUPS, n)),
            dma((GROUPS,)),
            dma((GROUPS, nv)),
            dma((GROUPS, nv)),
            dma((n,)),
            dma((n,)),
            dma((chunks,)),
            dma((chunks,)),
            dma((GROUPS,)),
            dma((GROUPS,)),
            dma((GROUPS, chunks)),
            dma((GROUPS, chunks)),
            dma((GROUPS, chunks)),
            dma((GROUPS, chunks)),
            dma((GROUPS, chunks)),
        ],
        compiler_params=pltpu.CompilerParams(
            collective_id=0, has_side_effects=True, vmem_limit_bytes=50 * 1024 * 1024
        ),
        cost_estimate=pl.CostEstimate(
            flops=flops, bytes_accessed=2 * feat * (vloc + 2 * slots), transcendentals=3 * slots * vloc
        ),
        name="plan_loss",
    )(plan_lengths, shard_of_class, teacher_logprobs, hidden_rows, head_weight)
    return row_grad, row_kl.reshape(bal)


def solution(mesh):
    return jax.shard_map(
        body,
        mesh=mesh,
        in_specs=(P("dp", None), P(), P(), P(None, "vocab"), P("dp", "vocab")),
        out_specs=(P("dp", None), P("dp")),
        check_vma=False,
    )
```
